512 devices in a mesh: rows: 64 (over z, x), sub: 8 (over y, core).
Axes of the slice: x: 4, y: 4, z: 16, core: 2. Of those that a mesh axis runs over, the one named last changes fastest.
Arguments:
- basis: float32 [8, 64, 131072], P(None, None, ('rows', 'sub'))
- stiffness: float32 [12, 8, 8, 131072], P(None, None, None, ('rows', 'sub')), as said below
- col_index: int32 [12, 131072], P(None, ('rows', 'sub')), may hold values from 0 to 319, as said below
- block_count: int32 [131072], P(('rows', 'sub')), may hold values from 6 to 12, as said below
- send_list: int32 [2, 16384], P(None, ('rows', 'sub')), may hold values from 0 to 255, as said below
Outputs:
- basis_next: float32 [8, 64, 131072], P(None, None, ('rows', 'sub'))
- factor: float32 [64, 64], replicated
The draws below stay inside these ranges and needn't reach their ends.
Inputs may be any that keep to these rules, and one draw needn't show every extreme that they name: col_index[0, b] is block row b's own slab-local index. A value v below 256 is a block row of the same slab; 256 + j is the j-th row of the previous slab's send_list[1]; 288 + j is the j-th row of the next slab's send_list[0]. Slots of the first slab may name 256 to 287 and slots of the last slab may name 288 to 319; those ghosts are zeros. Block row b uses slots 0 to block_count[b] - 1; later slots are ignored. `send_list`: in each slab, row 0 holds 32 distinct block rows below 128; row 1 holds 32 distinct block rows at or above 128. stiffness[0, i, i, b] is at least 2.
All inputs are finite; a program needn't handle non-finite values.
Results may differ from the reference program's by a relative error of at most 0.0003.
Values sent between devices are 32-bit elements; how exact they have to be, the bound alone decides.
A program may use at most 128 MiB of HBM per device.

```python
import math
import jax
import jax.numpy as jnp
from jax import lax

BLOCK = 8
LOADS = 64
SLOTS = 12
BROWS_DEV = 256
RIM = 128
SEND = 32
SLABS = 512
BROWS = 131072
ROWS = 1048576


def draw_basis(key, part):
    key = jax.random.fold_in(key, 1)
    key_rows, key_loads, key_base = jax.random.split(key, 3)
    position = jnp.arange(BROWS).astype(jnp.float32)
    trend = jnp.exp(math.log(3.0) * position / max(BROWS - 1, 1))
    row_scale = jnp.exp(jax.random.uniform(key_rows, (BROWS,), jnp.float32, 0.0, math.log(10.0))) * trend
    load_scale = jnp.exp(jax.random.uniform(key_loads, (LOADS,), jnp.float32, 0.0, math.log(10.0)))
    base = jax.random.normal(key_base, (BLOCK, LOADS, BROWS), jnp.float32)
    return 0.25 * base * load_scale[None, :, None] * row_scale[None, None, :]


def draw_stiffness(key, part):
    key = jax.random.fold_in(key, 2)
    key_off, key_diag = jax.random.split(key, 2)
    off_part = jax.random.uniform(key_off, (SLOTS, BLOCK, BLOCK, BROWS), jnp.float32, -0.4, 0.4)
    pivot_part = jax.random.uniform(key_diag, (BLOCK, BROWS), jnp.float32, 3.0, 8.0)
    identity = (jnp.arange(BLOCK)[:, None] == jnp.arange(BLOCK)[None, :]).astype(jnp.float32)
    first = (jnp.arange(SLOTS) == 0).astype(jnp.float32)
    return off_part + first[:, None, None, None] * identity[None, :, :, None] * pivot_part[None, :, None, :]


def draw_col_index(key, part):
    key = jax.random.fold_in(key, 3)
    key_off, key_ghost = jax.random.split(key, 2)
    local_row = jnp.arange(BROWS, dtype=jnp.int32) % BROWS_DEV
    offset = jax.random.randint(key_off, (SLOTS, BROWS), -RIM, RIM + 1, jnp.int32)
    target = local_row[None, :] + offset
    ghost = jax.random.randint(key_ghost, (SLOTS, BROWS), 0, SEND, jnp.int32)
    column = jnp.where(target < 0, BROWS_DEV + ghost, jnp.where(target >= BROWS_DEV, BROWS_DEV + SEND + ghost, target))
    slot_ids = jnp.arange(SLOTS, dtype=jnp.int32)[:, None]
    column = jnp.where(slot_ids == 0, local_row[None, :], column)
    forced = (slot_ids == 1) & (local_row[None, :] == BROWS_DEV - 1)
    return jnp.where(forced, BROWS_DEV + 2 * SEND - 1, column).astype(jnp.int32)


def draw_block_count(key, part):
    key = jax.random.fold_in(key, 4)
    local_row = jnp.arange(BROWS, dtype=jnp.int32) % BROWS_DEV
    counts = jax.random.randint(key, (BROWS,), SLOTS // 2, SLOTS + 1, jnp.int32)
    counts = jnp.where((local_row == 0) | (local_row == BROWS_DEV - 1), SLOTS, counts)
    return jnp.where(local_row == 1, SLOTS // 2, counts).astype(jnp.int32)


def draw_send_list(key, part):
    key = jax.random.fold_in(key, 5)
    scores = jax.random.randint(key, (2, SLABS, RIM), 0, 2 ** 20, jnp.int32) * RIM + jnp.arange(RIM, dtype=jnp.int32)
    edge = jnp.stack([jnp.arange(RIM) == 0, jnp.arange(RIM) == RIM - 1]).astype(jnp.int32)
    scores = scores + edge[:, None, :] * 2 ** 28
    chosen = lax_top(scores)
    offset = jnp.array([0, BROWS_DEV - RIM], jnp.int32)
    return (chosen + offset[:, None, None]).reshape(2, SLABS * SEND).astype(jnp.int32)


def lax_top(scores):
    return jax.lax.top_k(scores, SEND)[1].astype(jnp.int32)


def setup_inputs(seed: int = 0) -> dict:
    seeds = jax.random.split(jax.random.key(seed), 6)
    basis = draw_basis(jax.random.fold_in(seeds[5], 71), 0)
    stiffness = draw_stiffness(jax.random.fold_in(seeds[5], 71), 0)
    col_index = draw_col_index(jax.random.fold_in(seeds[5], 71), 0)
    block_count = draw_block_count(jax.random.fold_in(seeds[5], 71), 0)
    send_list = draw_send_list(jax.random.fold_in(seeds[5], 71), 0)
    return dict(basis=basis, stiffness=stiffness, col_index=col_index, block_count=block_count, send_list=send_list)


def slab_product(extended, columns, counts, values):

    def add_slot(slot_idx, total):
        picked = jnp.take(extended, columns[slot_idx], axis=2)
        live_mask = (slot_idx < counts).astype(total.dtype)
        coefficient = values[slot_idx] * live_mask
        return total + jnp.einsum('ijb,jlb->ilb', coefficient, picked, precision=lax.Precision.HIGHEST)
    start = jnp.zeros((extended.shape[0], extended.shape[1], columns.shape[1]), jnp.float32)
    total = lax.fori_loop(0, columns.shape[0], add_slot, start.astype(extended.dtype))
    pivots = jnp.diagonal(values[0], axis1=0, axis2=1).T
    return total / pivots[:, None, :]

def reference(basis, stiffness, col_index, block_count, send_list):
    slabs = basis.shape[2] // BROWS_DEV
    blocks = jnp.moveaxis(basis.reshape(BLOCK, LOADS, slabs, BROWS_DEV), 2, 0)
    lists_all = send_list.reshape(2, slabs, SEND)
    pick_rows = jax.vmap(lambda field, chosen: jnp.take(field, chosen, axis=2))
    to_left = pick_rows(blocks, lists_all[0])
    to_right = pick_rows(blocks, lists_all[1])
    empty = jnp.zeros_like(to_left[:1])
    left_ghost = jnp.concatenate([empty, to_right[:-1]], axis=0)
    right_ghost = jnp.concatenate([to_left[1:], empty], axis=0)
    extended = jnp.concatenate([blocks, left_ghost, right_ghost], axis=3)
    columns = jnp.moveaxis(col_index.reshape(SLOTS, slabs, BROWS_DEV), 1, 0)
    counts = block_count.reshape(slabs, BROWS_DEV)
    values = jnp.moveaxis(stiffness.reshape(SLOTS, BLOCK, BLOCK, slabs, BROWS_DEV), 3, 0)
    scaled = lax.map(lambda items: slab_product(items[0], items[1], items[2], items[3]), (extended, columns, counts, values))
    matrix = jnp.transpose(scaled, (2, 0, 1, 3)).reshape(LOADS, -1)
    ortho, upper_factor = jnp.linalg.qr(matrix.T)
    signs = jnp.sign(jnp.diagonal(upper_factor))
    root = jnp.sqrt(jnp.asarray(ROWS, matrix.dtype))
    factor = upper_factor * signs[:, None] / root
    rows_out = (ortho * signs[None, :] * root).T.reshape(LOADS, slabs, BLOCK, BROWS_DEV)
    basis_next = jnp.transpose(rows_out, (2, 0, 1, 3)).reshape(BLOCK, LOADS, slabs * BROWS_DEV)
    return (basis_next, factor)
```

```python
import functools

import jax
import jax.numpy as jnp
from jax import lax
from jax.experimental import pallas as pl
from jax.experimental.pallas import tpu as pltpu
from jax.sharding import PartitionSpec as P

BLOCK = 8
LOADS = 64
SLOTS = 12
BROWS_DEV = 256
SEND = 32
CHIPS_X = 4
F32 = jnp.float32
BF16 = jnp.bfloat16
MESH = pl.DeviceIdType.MESH


def split3(value):
    high = value.astype(BF16)
    rest = value - high.astype(F32)
    mid = rest.astype(BF16)
    low = (rest - mid.astype(F32)).astype(BF16)
    return high, mid, low


def dot(a, b):
    return lax.dot_general(a, b, (((1,), (0,)), ((), ())), preferred_element_type=F32)


def one_hot(condition):
    return jnp.where(condition, 1.0, 0.0).astype(BF16)


def iota(shape, dim):
    return lax.broadcasted_iota(jnp.int32, shape, dim)


def factor_rows(M):
    M = list(M)
    outs = []
    full = (8, 128)
    for p in range(8):
        T = M[p]
        t = [jnp.broadcast_to(T[r : r + 1, :], full) for r in range(8)]
        s = {}
        for r in range(8):
            for m in range(r, 8):
                s[r, m] = jnp.broadcast_to(T[r : r + 1, 8 * p + m : 8 * p + m + 1], full)
        C = {}
        for q in range(p + 1, 8):
            for j in range(8):
                C[q, j] = jnp.broadcast_to(M[q][:, 8 * p + j : 8 * p + j + 1], full)
        inv, f, u = [], {}, []
        for j in range(8):
            r = lax.rsqrt(s[j, j])
            inv.append(r)
            for m in range(j + 1, 8):
                f[j, m] = s[j, m] * r
            u.append(t[j] * r)
            for m in range(j + 1, 8):
                for n in range(m, 8):
                    s[m, n] = s[m, n] - f[j, m] * f[j, n]
                t[m] = t[m] - f[j, m] * u[j]
        outs.append(u)
        if p == 7:
            break
        v = [None] * 8
        for j in range(7, -1, -1):
            a = u[j]
            for m in range(j + 1, 8):
                a = a - f[j, m] * v[m]
            v[j] = a * inv[j]
        for q in range(p + 1, 8):
            parts = [C[q, j] * v[j] for j in range(8)]
            while len(parts) > 1:
                parts = [parts[i] + parts[i + 1] for i in range(0, len(parts), 2)]
            M[q] = M[q] - parts[0]
    return outs


def kernel(nz, ny2, basis_ref, stiff_ref, cols_ref, count_ref, list_ref, out_ref, factor_ref,
           x_ref, s_ref, xt_ref, cc_ref, pick_ref, acc_ref, wt_ref, gst_ref,
           halo_out, halo_in, plane_out, plane_in, z_out, z_in, core_out, core_in, rows_ref,
           load_sem, halo_sem, plane_sem, z_sem, core_sem):
    nx = CHIPS_X
    rows = lax.axis_index("rows")
    sub = lax.axis_index("sub")
    z, x = rows // nx, rows % nx
    core = sub % 2
    slabs = nz * nx * ny2
    slab = rows * ny2 + sub
    nplane = nx * ny2
    me_plane = x * ny2 + sub

    def flat(index):
        return (index // ny2, index % ny2)

    prev_id, next_id = flat((slab + slabs - 1) % slabs), flat((slab + 1) % slabs)

    def plane_id(index):
        return (z * nx + index // ny2, index % ny2)

    def z_id(index):
        return (index * nx + x, sub)

    barrier = pltpu.get_barrier_semaphore()

    def greet(device):
        pl.semaphore_signal(barrier, inc=1, device_id=device, device_id_type=MESH)

    load_x = pltpu.make_async_copy(basis_ref, x_ref, load_sem.at[0])
    load_s = pltpu.make_async_copy(stiff_ref, s_ref, load_sem.at[1])
    load_x.start()
    load_s.start()
    greet(prev_id)
    greet(next_id)

    def greet_z(q, carry):
        greet(z_id((z + q) % nz))
        return carry

    def greet_plane(q, carry):
        greet(plane_id((me_plane + q) % nplane))
        return carry

    lax.fori_loop(1, nz, greet_z, 0)
    lax.fori_loop(1, nplane, greet_plane, 0)

    cols = cols_ref[...]
    live = iota(cols.shape, 0) < count_ref[...]
    from_prev = jnp.logical_and(cols >= BROWS_DEV, cols < BROWS_DEV + SEND)
    from_next = cols >= BROWS_DEV + SEND
    first = jnp.where(slab == 0, 1, 0)
    last = jnp.where(slab == slabs - 1, 1, 0)
    gone = jnp.where(from_prev, first, 0) + jnp.where(from_next, last, 0)
    cc_ref[...] = jnp.where(jnp.logical_and(live, gone == 0), cols, -1)

    load_x.wait()
    for j in range(BLOCK):
        for t, term in enumerate(split3(x_ref[j])):
            xt_ref[t, LOADS * j : LOADS * (j + 1), :] = term

    place = iota((BROWS_DEV, BROWS_DEV), 0)
    lane = iota((BROWS_DEV, BROWS_DEV), 1)
    lists = jnp.concatenate([list_ref[0:1, :]] * 4 + [list_ref[1:2, :]] * 4, axis=1)
    hit = place == lists
    packed = None
    for q in range(4):
        sel = one_hot(jnp.logical_and(hit, (lane % 128) // SEND == q))
        for t in range(3):
            term = dot(xt_ref[t, 128 * q : 128 * (q + 1), :], sel)
            packed = term if packed is None else packed + term
    halo_out[0] = packed[:, :128]
    halo_out[1] = packed[:, 128:]

    pl.semaphore_wait(barrier, 2 + (nz - 1) + (nplane - 1))
    to_prev = pltpu.make_async_remote_copy(
        src_ref=halo_out.at[0], dst_ref=halo_in.at[1], send_sem=halo_sem.at[0],
        recv_sem=halo_sem.at[1], device_id=prev_id, device_id_type=MESH)
    to_next = pltpu.make_async_remote_copy(
        src_ref=halo_out.at[1], dst_ref=halo_in.at[0], send_sem=halo_sem.at[2],
        recv_sem=halo_sem.at[3], device_id=next_id, device_id_type=MESH)
    to_prev.start()
    to_next.start()

    def pick_local(k, carry):
        sel = one_hot(place == cc_ref[pl.ds(k, 1), :])
        got = dot(xt_ref[0], sel) + dot(xt_ref[1], sel) + dot(xt_ref[2], sel)
        pick_ref[k] = got.reshape(BLOCK, LOADS, BROWS_DEV)
        return carry

    lax.fori_loop(1, SLOTS, pick_local, 0)
    load_s.wait()

    def multiply(k, source, start):
        for c in range(2):
            lanes = slice(128 * c, 128 * (c + 1))
            for h in range(2):
                loads = slice(32 * h, 32 * (h + 1))
                total = None if start else acc_ref[:, loads, lanes]
                for j in range(BLOCK):
                    term = s_ref[k, :, j : j + 1, lanes] * source(j, loads, lanes)[None]
                    total = term if total is None else total + term
                acc_ref[:, loads, lanes] = total

    multiply(0, lambda j, loads, lanes: x_ref[j, loads, lanes], True)

    to_prev.wait_recv()
    to_next.wait_recv()
    sides = [split3(halo_in[0]), split3(halo_in[1])]
    r = iota((BROWS_DEV, 192), 0)
    n = iota((BROWS_DEV, 192), 1)
    for q in range(4):
        total = None
        for t in range(3):
            want = (n % 64) // SEND * 128 + SEND * q + n % SEND
            sel = one_hot(jnp.logical_and(n // 64 == t, r == want))
            term = dot(sides[0][t], sel[:128]) + dot(sides[1][t], sel[128:])
            total = term if total is None else total + term
        gst_ref[128 * q : 128 * (q + 1), :] = total.astype(BF16)

    ghost_place = BROWS_DEV + iota((192, BROWS_DEV), 0) % 64

    def slot(k, carry):
        sel = one_hot(ghost_place == cc_ref[pl.ds(k, 1), :])
        got = dot(gst_ref[...], sel).reshape(BLOCK, LOADS, BROWS_DEV)
        pick_ref[k] = pick_ref[k] + got
        multiply(k, lambda j, loads, lanes: pick_ref[k, j, loads, lanes], False)
        return carry

    lax.fori_loop(1, SLOTS, slot, 0)

    gram = None
    for i in range(BLOCK):
        scaled = acc_ref[i] / s_ref[0, i, i : i + 1, :]
        wt_ref[i] = jnp.concatenate(split3(scaled), axis=0)
        term = lax.dot_general(wt_ref[i], wt_ref[i], (((1,), (1,)), ((), ())),
                               preferred_element_type=F32)
        gram = term if gram is None else gram + term
    gram = gram[0:64] + gram[64:128] + gram[128:192]
    gram = gram[:, 0:64] + gram[:, 64:128] + gram[:, 128:192]
    gram = gram * (1.0 / (BLOCK * BROWS_DEV * slabs))

    for c in range(2):
        plane_out[c] = jnp.concatenate([gram[32 * c : 32 * c + 16], gram[32 * c + 16 : 32 * c + 32]], axis=1)
    plane_in[me_plane] = plane_out[core]

    def send_plane(q, carry):
        to = (me_plane + q) % nplane
        pltpu.make_async_remote_copy(
            src_ref=plane_out.at[to % 2], dst_ref=plane_in.at[me_plane], send_sem=plane_sem.at[0],
            recv_sem=plane_sem.at[1], device_id=plane_id(to), device_id_type=MESH).start()
        return carry

    lax.fori_loop(1, nplane, send_plane, 0)
    part = plane_in.at[pl.ds(0, nplane - 1)]
    plane_all = pltpu.make_async_remote_copy(
        src_ref=part, dst_ref=part, send_sem=plane_sem.at[0], recv_sem=plane_sem.at[1],
        device_id=plane_id((me_plane + 1) % nplane), device_id_type=MESH)
    plane_all.wait_recv()
    total = jnp.sum(plane_in[...], axis=0)
    z_out[...] = total
    z_in[z] = total

    def send_z(q, carry):
        to = (z + q) % nz
        pltpu.make_async_remote_copy(
            src_ref=z_out, dst_ref=z_in.at[z], send_sem=z_sem.at[0],
            recv_sem=z_sem.at[1], device_id=z_id(to), device_id_type=MESH).start()
        return carry

    lax.fori_loop(1, nz, send_z, 0)
    part = z_in.at[pl.ds(0, nz - 1)]
    z_all = pltpu.make_async_remote_copy(
        src_ref=part, dst_ref=part, send_sem=z_sem.at[0], recv_sem=z_sem.at[1],
        device_id=z_id((z + 1) % nz), device_id_type=MESH)
    z_all.wait_recv()
    total = jnp.sum(z_in[...], axis=0)
    core_out[...] = total
    core_in[core] = total
    to_core = pltpu.make_async_remote_copy(
        src_ref=core_out, dst_ref=core_in.at[core], send_sem=core_sem.at[0],
        recv_sem=core_sem.at[1], device_id=(rows, sub + 1 - 2 * core), device_id_type=MESH)
    to_core.start()
    to_core.wait_recv()

    eye = jnp.where(iota((16, 64), 1) == iota((16, 64), 0), 1.0, 0.0)
    blocks = []
    for c in range(2):
        half = core_in[c]
        for g in range(2):
            base = 32 * c + 16 * g
            unit = jnp.where(iota((16, 64), 1) == iota((16, 64), 0) + base, 1.0, 0.0)
            both = jnp.concatenate([half[:, 64 * g : 64 * (g + 1)], unit], axis=1)
            blocks += [both[0:8], both[8:16]]
    outs = factor_rows(blocks)
    for p in range(8):
        for j in range(8):
            rows_ref[8 * p + j : 8 * p + j + 1, :] = outs[p][j][0:1]
    found = rows_ref[...]
    upper = iota((64, 64), 0) <= iota((64, 64), 1)
    factor_ref[...] = jnp.where(upper, found[:, :64], 0.0)
    left = jnp.concatenate([jnp.concatenate([term] * 3, axis=1) for term in split3(found[:, 64:])], axis=0)
    for i in range(BLOCK):
        got = dot(left, wt_ref[i])
        out_ref[i] = got[0:64] + got[64:128] + got[128:192]

    to_prev.wait_send()
    to_next.wait_send()
    plane_all.wait_send()
    z_all.wait_send()
    to_core.wait_send()


def on_device(nz, ny2, basis, stiffness, col_index, block_count, send_list):
    nplane = CHIPS_X * ny2
    vmem = pl.BlockSpec(memory_space=pltpu.VMEM)
    hbm = pl.BlockSpec(memory_space=pl.ANY)
    return pl.pallas_call(
        functools.partial(kernel, nz, ny2),
        out_shape=(jax.ShapeDtypeStruct(basis.shape, F32), jax.ShapeDtypeStruct((LOADS, LOADS), F32)),
        in_specs=[hbm, hbm, vmem, vmem, vmem],
        out_specs=(vmem, vmem),
        scratch_shapes=[
            pltpu.VMEM((BLOCK, LOADS, BROWS_DEV), F32),
            pltpu.VMEM((SLOTS, BLOCK, BLOCK, BROWS_DEV), F32),
            pltpu.VMEM((3, BLOCK * LOADS, BROWS_DEV), BF16),
            pltpu.VMEM((SLOTS, BROWS_DEV), jnp.int32),
            pltpu.VMEM((SLOTS, BLOCK, LOADS, BROWS_DEV), F32),
            pltpu.VMEM((BLOCK, LOADS, BROWS_DEV), F32),
            pltpu.VMEM((BLOCK, 3 * LOADS, BROWS_DEV), BF16),
            pltpu.VMEM((BLOCK * LOADS, 192), BF16),
            pltpu.VMEM((2, 128, 128), F32),
            pltpu.VMEM((2, 128, 128), F32),
            pltpu.VMEM((2, 16, 128), F32),
            pltpu.VMEM((nplane, 16, 128), F32),
            pltpu.VMEM((16, 128), F32),
            pltpu.VMEM((nz, 16, 128), F32),
            pltpu.VMEM((16, 128), F32),
            pltpu.VMEM((2, 16, 128), F32),
            pltpu.VMEM((LOADS, 128), F32),
            pltpu.SemaphoreType.DMA((2,)),
            pltpu.SemaphoreType.DMA((4,)),
            pltpu.SemaphoreType.DMA((2,)),
            pltpu.SemaphoreType.DMA((2,)),
            pltpu.SemaphoreType.DMA((2,)),
        ],
        name="arnoldi_step",
        compiler_params=pltpu.CompilerParams(
            collective_id=1, has_side_effects=True, vmem_limit_bytes=48 * 1024 * 1024),
    )(basis, stiffness, col_index, block_count.reshape(1, BROWS_DEV), send_list)


def solution(mesh):
    nz, ny2 = mesh.shape["rows"] // CHIPS_X, mesh.shape["sub"]
    in_specs = (
        P(None, None, ("rows", "sub")),
        P(None, None, None, ("rows", "sub")),
        P(None, ("rows", "sub")),
        P(("rows", "sub")),
        P(None, ("rows", "sub")),
    )
    out_specs = (P(None, None, ("rows", "sub")), P())
    return jax.shard_map(
        functools.partial(on_device, nz, ny2), mesh=mesh, in_specs=in_specs, out_specs=out_specs,
        check_vma=False,
    )
```

```python
import functools

import jax
import jax.numpy as jnp
from jax import lax
from jax.experimental import pallas as pl
from jax.experimental.pallas import tpu as pltpu
from jax.sharding import PartitionSpec as P

BLOCK = 8
LOADS = 64
SLOTS = 12
BROWS_DEV = 256
SEND = 32
CHIPS_X = 4
F32 = jnp.float32
BF16 = jnp.bfloat16
MESH = pl.DeviceIdType.MESH


def split3(value):
    high = value.astype(BF16)
    rest = value - high.astype(F32)
    mid = rest.astype(BF16)
    low = (rest - mid.astype(F32)).astype(BF16)
    return high, mid, low


def dot(a, b):
    return lax.dot_general(a, b, (((1,), (0,)), ((), ())), preferred_element_type=F32)


def one_hot(condition):
    return jnp.where(condition, 1.0, 0.0).astype(BF16)


def iota(shape, dim):
    return lax.broadcasted_iota(jnp.int32, shape, dim)


def factor_rows(M):
    M = list(M)
    outs = []
    full = (8, 128)
    for p in range(8):
        T = M[p]
        t = [jnp.broadcast_to(T[r : r + 1, :], full) for r in range(8)]
        s = {}
        for r in range(8):
            for m in range(r, 8):
                s[r, m] = jnp.broadcast_to(T[r : r + 1, 8 * p + m : 8 * p + m + 1], full)
        C = {}
        for q in range(p + 1, 8):
            for j in range(8):
                C[q, j] = jnp.broadcast_to(M[q][:, 8 * p + j : 8 * p + j + 1], full)
        inv, f, u = [], {}, []
        for j in range(8):
            r = lax.rsqrt(s[j, j])
            inv.append(r)
            for m in range(j + 1, 8):
                f[j, m] = s[j, m] * r
            u.append(t[j] * r)
            for m in range(j + 1, 8):
                for n in range(m, 8):
                    s[m, n] = s[m, n] - f[j, m] * f[j, n]
                t[m] = t[m] - f[j, m] * u[j]
        outs.append(u)
        if p == 7:
            break
        v = [None] * 8
        for j in range(7, -1, -1):
            a = u[j]
            for m in range(j + 1, 8):
                a = a - f[j, m] * v[m]
            v[j] = a * inv[j]
        for q in range(p + 1, 8):
            parts = [C[q, j] * v[j] for j in range(8)]
            while len(parts) > 1:
                parts = [parts[i] + parts[i + 1] for i in range(0, len(parts), 2)]
            M[q] = M[q] - parts[0]
    return outs


def kernel(nz, ny2, basis_ref, stiff_ref, cols_hbm, count_hbm, list_hbm, wt_ref, sum_ref,
           x_ref, s_ref, cols_ref, count_ref, list_ref, xt_ref, cc_ref, pick_ref, acc_ref, gst_ref,
           halo_out, halo_in, plane_out, plane_in, z_out, z_in, core_out,
           load_sem, halo_sem, plane_sem, z_sem, core_sem, near_sem, far_sem):
    nx = CHIPS_X
    rows = lax.axis_index("rows")
    sub = lax.axis_index("sub")
    z, x = rows // nx, rows % nx
    core = sub % 2
    slabs = nz * nx * ny2
    slab = rows * ny2 + sub
    nplane = nx * ny2
    me_plane = x * ny2 + sub

    def flat(index):
        return (index // ny2, index % ny2)

    prev_id, next_id = flat((slab + slabs - 1) % slabs), flat((slab + 1) % slabs)

    def z_id(index):
        return (index * nx + x, sub)

    barrier = pltpu.get_barrier_semaphore()

    def greet(device):
        pl.semaphore_signal(barrier, inc=1, device_id=device, device_id_type=MESH)

    load_x = pltpu.make_async_copy(basis_ref, x_ref, load_sem.at[0])
    load_s = pltpu.make_async_copy(stiff_ref, s_ref, load_sem.at[1])
    load_c = pltpu.make_async_copy(cols_hbm, cols_ref, load_sem.at[2])
    load_n = pltpu.make_async_copy(count_hbm, count_ref, load_sem.at[3])
    load_l = pltpu.make_async_copy(list_hbm, list_ref, load_sem.at[4])
    load_l.start()
    load_x.start()
    load_c.start()
    load_n.start()
    load_s.start()
    greet(prev_id)
    greet(next_id)
    for q in range(1, ny2):
        greet((rows, (sub + q) % ny2))
    x_peers = [(z * nx + (x + q) % nx, sub) for q in range(1, nx)]
    for peer in x_peers:
        greet(peer)
    greet(z_id((z + 1) % nz))
    greet(z_id((z + nz - 1) % nz))

    load_c.wait()
    load_n.wait()
    cols = cols_ref[...]
    live = iota(cols.shape, 0) < count_ref[...]
    from_prev = jnp.logical_and(cols >= BROWS_DEV, cols < BROWS_DEV + SEND)
    from_next = cols >= BROWS_DEV + SEND
    first = jnp.where(slab == 0, 1, 0)
    last = jnp.where(slab == slabs - 1, 1, 0)
    gone = jnp.where(from_prev, first, 0) + jnp.where(from_next, last, 0)
    cc_ref[...] = jnp.where(jnp.logical_and(live, gone == 0), cols, -1)

    load_l.wait()
    load_x.wait()
    for j in range(BLOCK):
        for t, term in enumerate(split3(x_ref[j])):
            xt_ref[t, LOADS * j : LOADS * (j + 1), :] = term

    place = iota((BROWS_DEV, BROWS_DEV), 0)
    lane = iota((BROWS_DEV, BROWS_DEV), 1)
    lists = jnp.concatenate([list_ref[0:1, :]] * 4 + [list_ref[1:2, :]] * 4, axis=1)
    hit = place == lists
    packed = None
    for q in range(4):
        sel = one_hot(jnp.logical_and(hit, (lane % 128) // SEND == q))
        for t in range(3):
            term = dot(xt_ref[t, 128 * q : 128 * (q + 1), :], sel)
            packed = term if packed is None else packed + term
    halo_out[0] = packed[:, :128]
    halo_out[1] = packed[:, 128:]

    pl.semaphore_wait(barrier, 2 + (ny2 - 1) + (nx - 1) + 2)
    to_prev = pltpu.make_async_remote_copy(
        src_ref=halo_out.at[0], dst_ref=halo_in.at[1], send_sem=halo_sem.at[0],
        recv_sem=halo_sem.at[1], device_id=prev_id, device_id_type=MESH)
    to_next = pltpu.make_async_remote_copy(
        src_ref=halo_out.at[1], dst_ref=halo_in.at[0], send_sem=halo_sem.at[2],
        recv_sem=halo_sem.at[3], device_id=next_id, device_id_type=MESH)
    to_prev.start()
    to_next.start()
    for peer in x_peers:
        pl.semaphore_signal(near_sem, inc=1, device_id=peer, device_id_type=MESH)

    def tell(step):
        for to in ((z + step) % nz, (z + nz - step) % nz):
            pl.semaphore_signal(far_sem.at[step.bit_length() - 1], inc=1, device_id=z_id(to), device_id_type=MESH)

    def hear(step):
        pl.semaphore_wait(far_sem.at[step.bit_length() - 1], 2)

    steps = [1 << e for e in range(8) if 2 * (1 << e) <= nz // 2]
    if steps:
        tell(steps[0])

    def pick_local(k, carry):
        sel = one_hot(place == cc_ref[pl.ds(k, 1), :])
        got = dot(xt_ref[0], sel) + dot(xt_ref[1], sel) + dot(xt_ref[2], sel)
        pick_ref[k] = got.reshape(BLOCK, LOADS, BROWS_DEV)
        return carry

    lax.fori_loop(1, SLOTS, pick_local, 0)
    load_s.wait()

    def multiply(k, source, start):
        for c in range(2):
            lanes = slice(128 * c, 128 * (c + 1))
            for h in range(2):
                loads = slice(32 * h, 32 * (h + 1))
                total = None if start else acc_ref[:, loads, lanes]
                for j in range(BLOCK):
                    term = s_ref[k, :, j : j + 1, lanes] * source(j, loads, lanes)[None]
                    total = term if total is None else total + term
                acc_ref[:, loads, lanes] = total

    multiply(0, lambda j, loads, lanes: x_ref[j, loads, lanes], True)

    to_prev.wait_recv()
    to_next.wait_recv()
    if len(steps) > 1:
        hear(steps[0])
        tell(steps[1])
    sides = [split3(halo_in[0]), split3(halo_in[1])]
    r = iota((BROWS_DEV, 192), 0)
    n = iota((BROWS_DEV, 192), 1)
    for q in range(4):
        total = None
        for t in range(3):
            want = (n % 64) // SEND * 128 + SEND * q + n % SEND
            sel = one_hot(jnp.logical_and(n // 64 == t, r == want))
            term = dot(sides[0][t], sel[:128]) + dot(sides[1][t], sel[128:])
            total = term if total is None else total + term
        gst_ref[128 * q : 128 * (q + 1), :] = total.astype(BF16)

    ghost_place = BROWS_DEV + iota((192, BROWS_DEV), 0) % 64

    def add_ghosts(k, carry):
        sel = one_hot(ghost_place == cc_ref[pl.ds(k, 1), :])
        got = dot(gst_ref[...], sel).reshape(BLOCK, LOADS, BROWS_DEV)
        pick_ref[k] = pick_ref[k] + got
        return carry

    lax.fori_loop(1, SLOTS, add_ghosts, 0)
    for c in range(2):
        lanes = slice(128 * c, 128 * (c + 1))
        for h in range(2):
            loads = slice(32 * h, 32 * (h + 1))

            def slot(k, total):
                for j in range(BLOCK):
                    total = total + s_ref[k, :, j : j + 1, lanes] * pick_ref[k, j, loads, lanes][None]
                return total

            acc_ref[:, loads, lanes] = lax.fori_loop(1, SLOTS, slot, acc_ref[:, loads, lanes])

    gram = None
    for i in range(BLOCK):
        scaled = acc_ref[i] / s_ref[0, i, i : i + 1, :]
        wt_ref[i] = jnp.concatenate(split3(scaled), axis=0)
        term = lax.dot_general(wt_ref[i], wt_ref[i], (((1,), (1,)), ((), ())),
                               preferred_element_type=F32)
        gram = term if gram is None else gram + term
    gram = gram[0:64] + gram[64:128] + gram[128:192]
    gram = gram[:, 0:64] + gram[:, 64:128] + gram[:, 128:192]
    gram = gram * (1.0 / (BLOCK * BROWS_DEV * slabs))

    pack(plane_out, gram)
    pl.semaphore_wait(near_sem, nx - 1)
    plane_in[me_plane] = plane_out[core]

    for dx in (2, 1, 3, 0):
        for dy in range(ny2):
            shift = (ny2 // 2 + dy) % ny2
            if dx or shift:
                to_x, to_sub = (x + dx) % nx, (sub + shift) % ny2
                pltpu.make_async_remote_copy(
                    src_ref=plane_out.at[to_sub % 2], dst_ref=plane_in.at[me_plane],
                    send_sem=plane_sem.at[0], recv_sem=plane_sem.at[1],
                    device_id=(z * nx + to_x, to_sub), device_id_type=MESH).start()

    for e in range(1, len(steps) - 1):
        hear(steps[e])
        tell(steps[e + 1])
    part = plane_in.at[pl.ds(0, nplane - 1)]
    plane_all = pltpu.make_async_remote_copy(
        src_ref=part, dst_ref=part, send_sem=plane_sem.at[0], recv_sem=plane_sem.at[1],
        device_id=(rows, sub + 1 - 2 * core), device_id_type=MESH)
    plane_all.wait_recv()
    total = jnp.sum(plane_in[...], axis=0)
    z_out[...] = total
    z_in[z] = total

    if steps:
        hear(steps[-1])

    def send_z(q, carry):
        half = (q + 1) // 2
        to = (z + nz // 2 + half * (1 - 2 * (q % 2))) % nz
        pltpu.make_async_remote_copy(
            src_ref=z_out, dst_ref=z_in.at[z], send_sem=z_sem.at[0],
            recv_sem=z_sem.at[1], device_id=z_id(to), device_id_type=MESH).start()
        return carry

    lax.fori_loop(0, nz - 1, send_z, 0)
    part = z_in.at[pl.ds(0, nz - 1)]
    z_all = pltpu.make_async_remote_copy(
        src_ref=part, dst_ref=part, send_sem=z_sem.at[0], recv_sem=z_sem.at[1],
        device_id=z_id((z + 1) % nz), device_id_type=MESH)
    z_all.wait_recv()
    total = jnp.sum(z_in[...], axis=0)
    core_out[...] = total
    sum_ref[core] = total
    to_core = pltpu.make_async_remote_copy(
        src_ref=core_out, dst_ref=sum_ref.at[core], send_sem=core_sem.at[0],
        recv_sem=core_sem.at[1], device_id=(rows, sub + 1 - 2 * core), device_id_type=MESH)
    to_core.start()
    to_core.wait_recv()

    to_prev.wait_send()
    to_next.wait_send()
    plane_all.wait_send()
    z_all.wait_send()
    to_core.wait_send()


def pack(ref, gram):
    wide = [gram[0:16], jnp.concatenate([gram[16:32, 16:64], gram[32:48, 32:48]], axis=1)]
    small = [gram[48:64, 48:64], gram[32:48, 48:64]]
    for c in range(2):
        ref[c, 0:8, :] = jnp.concatenate([wide[c][0:8], wide[c][8:16]], axis=1)
        ref[c, 8:10, :] = jnp.concatenate([small[c][2 * i : 2 * i + 2] for i in range(8)], axis=1)


def unpack(ref):
    wide = [jnp.concatenate([ref[c, 0:8, 0:64], ref[c, 0:8, 64:128]], axis=0) for c in range(2)]
    small = [jnp.concatenate([ref[c, 8:10, 16 * i : 16 * (i + 1)] for i in range(8)], axis=0) for c in range(2)]
    zeros = jnp.zeros((16, 48), F32)
    rows = [
        wide[0],
        jnp.concatenate([zeros[:, 0:16], wide[1][:, 0:48]], axis=1),
        jnp.concatenate([zeros[:, 0:32], wide[1][:, 48:64], small[1]], axis=1),
        jnp.concatenate([zeros, small[0]], axis=1),
    ]
    upper = jnp.concatenate(rows, axis=0)
    keep = iota((LOADS, LOADS), 0) <= iota((LOADS, LOADS), 1)
    return jnp.where(keep, upper, upper.T)


def apply_kernel(wt_ref, sum_ref, out_hbm, factor_hbm, out_ref, factor_ref, rows_ref, sems):
    gram = unpack(sum_ref)
    unit = jnp.where(iota((LOADS, LOADS), 0) == iota((LOADS, LOADS), 1), 1.0, 0.0)
    both = jnp.concatenate([gram, unit], axis=1)
    outs = factor_rows([both[8 * p : 8 * p + 8] for p in range(8)])
    for p in range(8):
        for j in range(8):
            rows_ref[8 * p + j : 8 * p + j + 1, :] = outs[p][j][0:1]
    found = rows_ref[...]
    upper = iota((LOADS, LOADS), 0) <= iota((LOADS, LOADS), 1)
    factor_ref[...] = jnp.where(upper, found[:, :LOADS], 0.0)
    store = pltpu.make_async_copy(factor_ref, factor_hbm, sems.at[BLOCK])
    store.start()
    stores = [store]
    left = jnp.concatenate([jnp.concatenate([term] * 3, axis=1) for term in split3(found[:, LOADS:])], axis=0)
    for i in range(BLOCK):
        got = dot(left, wt_ref[i])
        out_ref[i] = got[0:64] + got[64:128] + got[128:192]
        store = pltpu.make_async_copy(out_ref.at[i], out_hbm.at[i], sems.at[i])
        store.start()
        stores.append(store)
    for store in stores:
        store.wait()


def on_device(nz, ny2, basis, stiffness, col_index, block_count, send_list):
    nplane = CHIPS_X * ny2
    vmem = pl.BlockSpec(memory_space=pltpu.VMEM)
    hbm = pl.BlockSpec(memory_space=pltpu.MemorySpace.HBM)
    held = [
        pltpu.with_memory_space_constraint(value, pltpu.MemorySpace.HBM)
        for value in (basis, stiffness, col_index, block_count.reshape(1, BROWS_DEV), send_list)
    ]
    wt, total = pl.pallas_call(
        functools.partial(kernel, nz, ny2),
        out_shape=(
            jax.ShapeDtypeStruct((BLOCK, 3 * LOADS, BROWS_DEV), BF16),
            jax.ShapeDtypeStruct((2, 10, 128), F32),
        ),
        in_specs=[hbm, hbm, hbm, hbm, hbm],
        out_specs=(vmem, vmem),
        scratch_shapes=[
            pltpu.VMEM((BLOCK, LOADS, BROWS_DEV), F32),
            pltpu.VMEM((SLOTS, BLOCK, BLOCK, BROWS_DEV), F32),
            pltpu.VMEM((SLOTS, BROWS_DEV), jnp.int32),
            pltpu.VMEM((1, BROWS_DEV), jnp.int32),
            pltpu.VMEM((2, SEND), jnp.int32),
            pltpu.VMEM((3, BLOCK * LOADS, BROWS_DEV), BF16),
            pltpu.VMEM((SLOTS, BROWS_DEV), jnp.int32),
            pltpu.VMEM((SLOTS, BLOCK, LOADS, BROWS_DEV), F32),
            pltpu.VMEM((BLOCK, LOADS, BROWS_DEV), F32),
            pltpu.VMEM((BLOCK * LOADS, 192), BF16),
            pltpu.VMEM((2, 128, 128), F32),
            pltpu.VMEM((2, 128, 128), F32),
            pltpu.VMEM((2, 10, 128), F32),
            pltpu.VMEM((nplane, 10, 128), F32),
            pltpu.VMEM((10, 128), F32),
            pltpu.VMEM((nz, 10, 128), F32),
            pltpu.VMEM((10, 128), F32),
            pltpu.SemaphoreType.DMA((5,)),
            pltpu.SemaphoreType.DMA((4,)),
            pltpu.SemaphoreType.DMA((2,)),
            pltpu.SemaphoreType.DMA((2,)),
            pltpu.SemaphoreType.DMA((2,)),
            pltpu.SemaphoreType.REGULAR,
            pltpu.SemaphoreType.REGULAR((4,)),
        ],
        name="arnoldi_step",
        compiler_params=pltpu.CompilerParams(
            collective_id=1, has_side_effects=True, vmem_limit_bytes=40 * 1024 * 1024),
    )(*held)
    return pl.pallas_call(
        apply_kernel,
        out_shape=(jax.ShapeDtypeStruct(basis.shape, F32), jax.ShapeDtypeStruct((LOADS, LOADS), F32)),
        in_specs=[vmem, vmem],
        out_specs=(hbm, hbm),
        scratch_shapes=[
            pltpu.VMEM((BLOCK, LOADS, BROWS_DEV), F32),
            pltpu.VMEM((LOADS, LOADS), F32),
            pltpu.VMEM((LOADS, 128), F32),
            pltpu.SemaphoreType.DMA((BLOCK + 1,)),
        ],
        name="apply",
        compiler_params=pltpu.CompilerParams(vmem_limit_bytes=16 * 1024 * 1024),
    )(wt, total)


def solution(mesh):
    nz, ny2 = mesh.shape["rows"] // CHIPS_X, mesh.shape["sub"]
    in_specs = (
        P(None, None, ("rows", "sub")),
        P(None, None, None, ("rows", "sub")),
        P(None, ("rows", "sub")),
        P(("rows", "sub")),
        P(None, ("rows", "sub")),
    )
    out_specs = (P(None, None, ("rows", "sub")), P())
    return jax.shard_map(
        functools.partial(on_device, nz, ny2), mesh=mesh, in_specs=in_specs, out_specs=out_specs,
        check_vma=False,
    )
```

```python
import functools

import jax
import jax.numpy as jnp
from jax import lax
from jax.experimental import pallas as pl
from jax.experimental.pallas import tpu as pltpu
from jax.sharding import PartitionSpec as P

BLOCK = 8
LOADS = 64
SLOTS = 12
BROWS_DEV = 256
SEND = 32
CHIPS_X = 4
F32 = jnp.float32
BF16 = jnp.bfloat16
MESH = pl.DeviceIdType.MESH


def split3(value):
    high = value.astype(BF16)
    rest = value - high.astype(F32)
    mid = rest.astype(BF16)
    low = (rest - mid.astype(F32)).astype(BF16)
    return high, mid, low


def dot(a, b):
    return lax.dot_general(a, b, (((1,), (0,)), ((), ())), preferred_element_type=F32)


def one_hot(condition):
    return jnp.where(condition, 1.0, 0.0).astype(BF16)


def iota(shape, dim):
    return lax.broadcasted_iota(jnp.int32, shape, dim)


def factor_rows(M, cols_ref):
    M = list(M)
    outs = []
    full = (8, 128)
    for p in range(8):
        T = M[p]
        cols_ref[p, 8] = T
        C = {}
        for q in range(p, 8):
            for j in range(8):
                C[q, j] = jnp.broadcast_to(M[q][:, 8 * p + j : 8 * p + j + 1], full)
        for j in range(8):
            cols_ref[p, j] = C[p, j]
        t = [jnp.broadcast_to(cols_ref[p, 8, r : r + 1, :], full) for r in range(8)]
        s = {}
        for r in range(8):
            for m in range(r, 8):
                s[r, m] = jnp.broadcast_to(cols_ref[p, m, r : r + 1, :], full)
        inv, f, u = [], {}, []
        for j in range(8):
            r = lax.rsqrt(s[j, j])
            inv.append(r)
            for m in range(j + 1, 8):
                f[j, m] = s[j, m] * r
            u.append(t[j] * r)
            for m in range(j + 1, 8):
                for n in range(m, 8):
                    s[m, n] = s[m, n] - f[j, m] * f[j, n]
                t[m] = t[m] - f[j, m] * u[j]
        outs.append(u)
        if p == 7:
            break
        v = [None] * 8
        for j in range(7, -1, -1):
            a = u[j]
            for m in range(j + 1, 8):
                a = a - f[j, m] * v[m]
            v[j] = a * inv[j]
        for q in range(p + 1, 8):
            parts = [C[q, j] * v[j] for j in range(8)]
            while len(parts) > 1:
                parts = [parts[i] + parts[i + 1] for i in range(0, len(parts), 2)]
            M[q] = M[q] - parts[0]
    return outs


def kernel(nz, ny2, basis_ref, stiff_ref, cols_hbm, count_hbm, list_hbm, wt_ref, sum_ref,
           x_ref, s_ref, cols_ref, count_ref, list_ref, xt_ref, cc_ref, pick_ref, acc_ref, gst_ref, sel_ref,
           halo_out, halo_in, plane_out, plane_in, z_out, z_in, core_out,
           load_sem, halo_sem, plane_sem, z_sem, core_sem, near_sem, far_sem):
    nx = CHIPS_X
    rows = lax.axis_index("rows")
    sub = lax.axis_index("sub")
    z, x = rows // nx, rows % nx
    core = sub % 2
    slabs = nz * nx * ny2
    slab = rows * ny2 + sub
    nplane = nx * ny2
    me_plane = x * ny2 + sub

    def flat(index):
        return (index // ny2, index % ny2)

    prev_id, next_id = flat((slab + slabs - 1) % slabs), flat((slab + 1) % slabs)

    def z_id(index):
        return (index * nx + x, sub)

    barrier = pltpu.get_barrier_semaphore()

    def greet(device):
        pl.semaphore_signal(barrier, inc=1, device_id=device, device_id_type=MESH)

    load_x = pltpu.make_async_copy(basis_ref, x_ref, load_sem.at[0])
    load_s = pltpu.make_async_copy(stiff_ref, s_ref, load_sem.at[1])
    load_c = pltpu.make_async_copy(cols_hbm, cols_ref, load_sem.at[2])
    load_n = pltpu.make_async_copy(count_hbm, count_ref, load_sem.at[3])
    load_l = pltpu.make_async_copy(list_hbm, list_ref, load_sem.at[4])
    load_l.start()
    load_x.start()
    load_c.start()
    load_n.start()
    load_s.start()
    greet(prev_id)
    greet(next_id)
    for q in range(1, ny2):
        greet((rows, (sub + q) % ny2))
    x_peers = [(z * nx + (x + q) % nx, sub) for q in range(1, nx)]
    for peer in x_peers:
        greet(peer)
    greet(z_id((z + 1) % nz))
    greet(z_id((z + nz - 1) % nz))

    load_c.wait()
    load_n.wait()
    cols = cols_ref[...]
    live = iota(cols.shape, 0) < count_ref[...]
    from_prev = jnp.logical_and(cols >= BROWS_DEV, cols < BROWS_DEV + SEND)
    from_next = cols >= BROWS_DEV + SEND
    first = jnp.where(slab == 0, 1, 0)
    last = jnp.where(slab == slabs - 1, 1, 0)
    gone = jnp.where(from_prev, first, 0) + jnp.where(from_next, last, 0)
    cc_ref[...] = jnp.where(jnp.logical_and(live, gone == 0), cols, -1)

    load_l.wait()
    load_x.wait()
    for j in range(BLOCK):
        for t, term in enumerate(split3(x_ref[j])):
            xt_ref[t, LOADS * j : LOADS * (j + 1), :] = term

    place = iota((BROWS_DEV, BROWS_DEV), 0)
    lane = iota((BROWS_DEV, BROWS_DEV), 1)
    lists = jnp.concatenate([list_ref[0:1, :]] * 4 + [list_ref[1:2, :]] * 4, axis=1)
    hit = place == lists
    packed = None
    for q in range(4):
        sel = one_hot(jnp.logical_and(hit, (lane % 128) // SEND == q))
        for t in range(3):
            term = dot(xt_ref[t, 128 * q : 128 * (q + 1), :], sel)
            packed = term if packed is None else packed + term
    halo_out[0] = packed[:, :128]
    halo_out[1] = packed[:, 128:]

    pl.semaphore_wait(barrier, 2 + (ny2 - 1) + (nx - 1) + 2)
    to_prev = pltpu.make_async_remote_copy(
        src_ref=halo_out.at[0], dst_ref=halo_in.at[1], send_sem=halo_sem.at[0],
        recv_sem=halo_sem.at[1], device_id=prev_id, device_id_type=MESH)
    to_next = pltpu.make_async_remote_copy(
        src_ref=halo_out.at[1], dst_ref=halo_in.at[0], send_sem=halo_sem.at[2],
        recv_sem=halo_sem.at[3], device_id=next_id, device_id_type=MESH)
    to_prev.start()
    to_next.start()
    for peer in x_peers:
        pl.semaphore_signal(near_sem, inc=1, device_id=peer, device_id_type=MESH)

    def tell(step):
        for to in ((z + step) % nz, (z + nz - step) % nz):
            pl.semaphore_signal(far_sem.at[step.bit_length() - 1], inc=1, device_id=z_id(to), device_id_type=MESH)

    def hear(step):
        pl.semaphore_wait(far_sem.at[step.bit_length() - 1], 2)

    steps = [1 << e for e in range(8) if 2 * (1 << e) <= nz // 2]
    if steps:
        tell(steps[0])

    def pick_local(k, carry):
        sel = one_hot(place == cc_ref[pl.ds(k, 1), :])
        got = dot(xt_ref[0], sel) + dot(xt_ref[1], sel) + dot(xt_ref[2], sel)
        pick_ref[k] = got.reshape(BLOCK, LOADS, BROWS_DEV)
        return carry

    lax.fori_loop(1, SLOTS, pick_local, 0)
    load_s.wait()
    if len(steps) > 1:
        hear(steps[0])
        tell(steps[1])

    def multiply(k, source, start):
        for c in range(2):
            lanes = slice(128 * c, 128 * (c + 1))
            for h in range(2):
                loads = slice(32 * h, 32 * (h + 1))
                total = None if start else acc_ref[:, loads, lanes]
                for j in range(BLOCK):
                    term = s_ref[k, :, j : j + 1, lanes] * source(j, loads, lanes)[None]
                    total = term if total is None else total + term
                acc_ref[:, loads, lanes] = total

    multiply(0, lambda j, loads, lanes: x_ref[j, loads, lanes], True)

    r = iota((BROWS_DEV, 192), 0)
    n = iota((BROWS_DEV, 192), 1)
    for q in range(4):
        want = (n % 64) // SEND * 128 + SEND * q + n % SEND
        for t in range(3):
            sel_ref[q, t] = one_hot(jnp.logical_and(n // 64 == t, r == want))

    to_prev.wait_recv()
    to_next.wait_recv()
    sides = [split3(halo_in[0]), split3(halo_in[1])]
    for q in range(4):
        total = None
        for t in range(3):
            term = dot(sides[0][t], sel_ref[q, t, :128]) + dot(sides[1][t], sel_ref[q, t, 128:])
            total = term if total is None else total + term
        gst_ref[128 * q : 128 * (q + 1), :] = total.astype(BF16)

    ghost_place = BROWS_DEV + iota((192, BROWS_DEV), 0) % 64

    def add_ghosts(k, carry):
        sel = one_hot(ghost_place == cc_ref[k : k + 1, :])
        got = dot(gst_ref[...], sel).reshape(BLOCK, LOADS, BROWS_DEV)
        pick_ref[k] = pick_ref[k] + got
        return carry

    for k in range(1, SLOTS):
        add_ghosts(k, 0)
    for c in range(2):
        lanes = slice(128 * c, 128 * (c + 1))

        for h in range(LOADS // 16):
            loads = slice(16 * h, 16 * (h + 1))

            def slot(k, total):
                for j in range(BLOCK):
                    total = total + s_ref[k, :, j : j + 1, lanes] * pick_ref[k, j, loads, lanes][None]
                return total

            acc_ref[:, loads, lanes] = lax.fori_loop(1, SLOTS, slot, acc_ref[:, loads, lanes])
        if c == 0 and len(steps) > 2:
            hear(steps[1])
            tell(steps[2])

    gram = None
    for i in range(BLOCK):
        scaled = acc_ref[i] / s_ref[0, i, i : i + 1, :]
        wt_ref[i] = jnp.concatenate(split3(scaled), axis=0)
        term = lax.dot_general(wt_ref[i], wt_ref[i], (((1,), (1,)), ((), ())),
                               preferred_element_type=F32)
        gram = term if gram is None else gram + term
    gram = gram[0:64] + gram[64:128] + gram[128:192]
    gram = gram[:, 0:64] + gram[:, 64:128] + gram[:, 128:192]
    gram = gram * (1.0 / (BLOCK * BROWS_DEV * slabs))

    pack(plane_out, gram)
    pl.semaphore_wait(near_sem, nx - 1)
    plane_in[me_plane] = plane_out[core]

    for dx in (2, 1, 3, 0):
        for dy in range(ny2):
            shift = (ny2 // 2 + dy) % ny2
            if dx or shift:
                to_x, to_sub = (x + dx) % nx, (sub + shift) % ny2
                pltpu.make_async_remote_copy(
                    src_ref=plane_out.at[to_sub % 2], dst_ref=plane_in.at[me_plane],
                    send_sem=plane_sem.at[0], recv_sem=plane_sem.at[1],
                    device_id=(z * nx + to_x, to_sub), device_id_type=MESH).start()

    part = plane_in.at[pl.ds(0, nplane - 1)]
    plane_all = pltpu.make_async_remote_copy(
        src_ref=part, dst_ref=part, send_sem=plane_sem.at[0], recv_sem=plane_sem.at[1],
        device_id=(rows, sub + 1 - 2 * core), device_id_type=MESH)
    plane_all.wait_recv()
    total = jnp.sum(plane_in[...], axis=0)
    z_out[...] = total
    z_in[z] = total

    if steps:
        hear(steps[-1])

    def send_z(q, carry):
        half = (q + 1) // 2
        to = (z + nz // 2 + half * (1 - 2 * (q % 2))) % nz
        pltpu.make_async_remote_copy(
            src_ref=z_out, dst_ref=z_in.at[z], send_sem=z_sem.at[0],
            recv_sem=z_sem.at[1], device_id=z_id(to), device_id_type=MESH).start()
        return carry

    lax.fori_loop(0, nz - 1, send_z, 0)
    part = z_in.at[pl.ds(0, nz - 1)]
    z_all = pltpu.make_async_remote_copy(
        src_ref=part, dst_ref=part, send_sem=z_sem.at[0], recv_sem=z_sem.at[1],
        device_id=z_id((z + 1) % nz), device_id_type=MESH)
    z_all.wait_recv()
    total = jnp.sum(z_in[...], axis=0)
    core_out[...] = total
    sum_ref[core] = total
    to_core = pltpu.make_async_remote_copy(
        src_ref=core_out, dst_ref=sum_ref.at[core], send_sem=core_sem.at[0],
        recv_sem=core_sem.at[1], device_id=(rows, sub + 1 - 2 * core), device_id_type=MESH)
    to_core.start()
    to_core.wait_recv()

    to_prev.wait_send()
    to_next.wait_send()
    plane_all.wait_send()
    z_all.wait_send()
    to_core.wait_send()


def pack(ref, gram):
    wide = [gram[0:16], jnp.concatenate([gram[16:32, 16:64], gram[32:48, 32:48]], axis=1)]
    small = [gram[48:64, 48:64], gram[32:48, 48:64]]
    for c in range(2):
        ref[c, 0:8, :] = jnp.concatenate([wide[c][0:8], wide[c][8:16]], axis=1)
        ref[c, 8:10, :] = jnp.concatenate([small[c][2 * i : 2 * i + 2] for i in range(8)], axis=1)


def unpack(ref):
    wide = [jnp.concatenate([ref[c, 0:8, 0:64], ref[c, 0:8, 64:128]], axis=0) for c in range(2)]
    small = [jnp.concatenate([ref[c, 8:10, 16 * i : 16 * (i + 1)] for i in range(8)], axis=0) for c in range(2)]
    zeros = jnp.zeros((16, 48), F32)
    rows = [
        wide[0],
        jnp.concatenate([zeros[:, 0:16], wide[1][:, 0:48]], axis=1),
        jnp.concatenate([zeros[:, 0:32], wide[1][:, 48:64], small[1]], axis=1),
        jnp.concatenate([zeros, small[0]], axis=1),
    ]
    upper = jnp.concatenate(rows, axis=0)
    keep = iota((LOADS, LOADS), 0) <= iota((LOADS, LOADS), 1)
    return jnp.where(keep, upper, upper.T)


def apply_kernel(wt_ref, sum_ref, out_hbm, factor_hbm, out_ref, factor_ref, rows_ref, cols_ref, sems):
    gram = unpack(sum_ref)
    unit = jnp.where(iota((LOADS, LOADS), 0) == iota((LOADS, LOADS), 1), 1.0, 0.0)
    both = jnp.concatenate([gram, unit], axis=1)
    outs = factor_rows([both[8 * p : 8 * p + 8] for p in range(8)], cols_ref)
    for p in range(8):
        for j in range(8):
            rows_ref[8 * p + j : 8 * p + j + 1, :] = outs[p][j][0:1]
    found = rows_ref[...]
    upper = iota((LOADS, LOADS), 0) <= iota((LOADS, LOADS), 1)
    factor_ref[...] = jnp.where(upper, found[:, :LOADS], 0.0)
    store = pltpu.make_async_copy(factor_ref, factor_hbm, sems.at[BLOCK])
    store.start()
    stores = [store]
    left = jnp.concatenate([jnp.concatenate([term] * 3, axis=1) for term in split3(found[:, LOADS:])], axis=0)
    for i in range(BLOCK):
        got = dot(left, wt_ref[i])
        out_ref[i] = got[0:64] + got[64:128] + got[128:192]
        store = pltpu.make_async_copy(out_ref.at[i], out_hbm.at[i], sems.at[i])
        store.start()
        stores.append(store)
    for store in stores:
        store.wait()


def on_device(nz, ny2, basis, stiffness, col_index, block_count, send_list):
    nplane = CHIPS_X * ny2
    vmem = pl.BlockSpec(memory_space=pltpu.VMEM)
    hbm = pl.BlockSpec(memory_space=pltpu.MemorySpace.HBM)
    held = [
        pltpu.with_memory_space_constraint(value, pltpu.MemorySpace.HBM)
        for value in (basis, stiffness, col_index, block_count.reshape(1, BROWS_DEV), send_list)
    ]
    wt, total = pl.pallas_call(
        functools.partial(kernel, nz, ny2),
        out_shape=(
            jax.ShapeDtypeStruct((BLOCK, 3 * LOADS, BROWS_DEV), BF16),
            jax.ShapeDtypeStruct((2, 10, 128), F32),
        ),
        in_specs=[hbm, hbm, hbm, hbm, hbm],
        out_specs=(vmem, vmem),
        scratch_shapes=[
            pltpu.VMEM((BLOCK, LOADS, BROWS_DEV), F32),
            pltpu.VMEM((SLOTS, BLOCK, BLOCK, BROWS_DEV), F32),
            pltpu.VMEM((SLOTS, BROWS_DEV), jnp.int32),
            pltpu.VMEM((1, BROWS_DEV), jnp.int32),
            pltpu.VMEM((2, SEND), jnp.int32),
            pltpu.VMEM((3, BLOCK * LOADS, BROWS_DEV), BF16),
            pltpu.VMEM((SLOTS, BROWS_DEV), jnp.int32),
            pltpu.VMEM((SLOTS, BLOCK, LOADS, BROWS_DEV), F32),
            pltpu.VMEM((BLOCK, LOADS, BROWS_DEV), F32),
            pltpu.VMEM((BLOCK * LOADS, 192), BF16),
            pltpu.VMEM((4, 3, BROWS_DEV, 192), BF16),
            pltpu.VMEM((2, 128, 128), F32),
            pltpu.VMEM((2, 128, 128), F32),
            pltpu.VMEM((2, 10, 128), F32),
            pltpu.VMEM((nplane, 10, 128), F32),
            pltpu.VMEM((10, 128), F32),
            pltpu.VMEM((nz, 10, 128), F32),
            pltpu.VMEM((10, 128), F32),
            pltpu.SemaphoreType.DMA((5,)),
            pltpu.SemaphoreType.DMA((4,)),
            pltpu.SemaphoreType.DMA((2,)),
            pltpu.SemaphoreType.DMA((2,)),
            pltpu.SemaphoreType.DMA((2,)),
            pltpu.SemaphoreType.REGULAR,
            pltpu.SemaphoreType.REGULAR((4,)),
        ],
        name="arnoldi_step",
        compiler_params=pltpu.CompilerParams(
            collective_id=1, has_side_effects=True, vmem_limit_bytes=40 * 1024 * 1024),
    )(*held)
    return pl.pallas_call(
        apply_kernel,
        out_shape=(jax.ShapeDtypeStruct(basis.shape, F32), jax.ShapeDtypeStruct((LOADS, LOADS), F32)),
        in_specs=[vmem, vmem],
        out_specs=(hbm, hbm),
        scratch_shapes=[
            pltpu.VMEM((BLOCK, LOADS, BROWS_DEV), F32),
            pltpu.VMEM((LOADS, LOADS), F32),
            pltpu.VMEM((LOADS, 128), F32),
            pltpu.VMEM((8, 9, 8, 128), F32),
            pltpu.SemaphoreType.DMA((BLOCK + 1,)),
        ],
        name="apply",
        compiler_params=pltpu.CompilerParams(vmem_limit_bytes=16 * 1024 * 1024),
    )(wt, total)


def solution(mesh):
    nz, ny2 = mesh.shape["rows"] // CHIPS_X, mesh.shape["sub"]
    in_specs = (
        P(None, None, ("rows", "sub")),
        P(None, None, None, ("rows", "sub")),
        P(None, ("rows", "sub")),
        P(("rows", "sub")),
        P(None, ("rows", "sub")),
    )
    out_specs = (P(None, None, ("rows", "sub")), P())
    return jax.shard_map(
        functools.partial(on_device, nz, ny2), mesh=mesh, in_specs=in_specs, out_specs=out_specs,
        check_vma=False,
    )
```

```python
import functools

import jax
import jax.numpy as jnp
from jax import lax
from jax.experimental import pallas as pl
from jax.experimental.pallas import tpu as pltpu
from jax.sharding import PartitionSpec as P

BLOCK = 8
LOADS = 64
SLOTS = 12
BROWS_DEV = 256
SEND = 32
CHIPS_X = 4
F32 = jnp.float32
BF16 = jnp.bfloat16
MESH = pl.DeviceIdType.MESH


def split3(value):
    high = value.astype(BF16)
    rest = value - high.astype(F32)
    mid = rest.astype(BF16)
    low = (rest - mid.astype(F32)).astype(BF16)
    return high, mid, low


def dot(a, b):
    return lax.dot_general(a, b, (((1,), (0,)), ((), ())), preferred_element_type=F32)


def one_hot(condition):
    return jnp.where(condition, 1.0, 0.0).astype(BF16)


def iota(shape, dim):
    return lax.broadcasted_iota(jnp.int32, shape, dim)


def factor_rows(M, cols_ref, near_ref):
    M = list(M)
    outs = []
    full = (8, 128)
    for p in range(8):
        T = M[p]
        cols_ref[p, 8] = T
        C = {}
        for q in range(p + 1, 8):
            for j in range(8):
                C[q, j] = jnp.broadcast_to(M[q][:, 8 * p + j : 8 * p + j + 1], full)
        if p == 0:
            corner = [jnp.broadcast_to(T[:, j : j + 1], full) for j in range(8)]
        for j in range(8):
            cols_ref[p, j] = corner[j]
        if p < 7:
            corner = [jnp.broadcast_to(M[p + 1][:, 8 * p + 8 + j : 8 * p + 9 + j], full) for j in range(8)]
        t = [jnp.broadcast_to(cols_ref[p, 8, r : r + 1, :], full) for r in range(8)]
        s = {}
        for r in range(8):
            for m in range(r, 8):
                s[r, m] = jnp.broadcast_to(cols_ref[p, m, r : r + 1, :], full)
        inv, f, u = [None] * 8, {}, [None] * 8
        near = [C[p + 1, j] for j in range(8)] if p < 7 else None
        for j in range(0, 8, 2):
            a, b = s[j, j], s[j, j + 1]
            first = lax.rsqrt(a)
            both = lax.rsqrt(a * s[j + 1, j + 1] - b * b)
            second = first * both
            inv[j], inv[j + 1] = first, a * first * both
            f[j, j + 1] = b * first
            for m in range(j + 2, 8):
                f[j, m] = s[j, m] * first
                f[j + 1, m] = (a * s[j + 1, m] - b * s[j, m]) * second
            u[j], u[j + 1] = t[j] * first, (a * t[j + 1] - b * t[j]) * second
            for m in range(j + 2, 8):
                for n in range(m, 8):
                    s[m, n] = s[m, n] - f[j, m] * f[j, n] - f[j + 1, m] * f[j + 1, n]
                t[m] = t[m] - f[j, m] * u[j] - f[j + 1, m] * u[j + 1]
            if near:
                e0, e1 = near[j] * first, (a * near[j + 1] - b * near[j]) * second
                for m in range(j + 2, 8):
                    near[m] = near[m] - f[j, m] * e0 - f[j + 1, m] * e1
                M[p + 1] = M[p + 1] - e0 * u[j] - e1 * u[j + 1]
                near_ref[p, j] = e0
                near_ref[p, j + 1] = e1
                for m in range(8):
                    d0 = jnp.broadcast_to(near_ref[p, j, m : m + 1, :], full)
                    d1 = jnp.broadcast_to(near_ref[p, j + 1, m : m + 1, :], full)
                    corner[m] = corner[m] - e0 * d0 - e1 * d1
        outs.append(u)
        if p >= 6:
            continue
        v = [None] * 8
        for j in range(7, -1, -1):
            a = u[j]
            for m in range(j + 1, 8):
                a = a - f[j, m] * v[m]
            v[j] = a * inv[j]
        for q in range(p + 2, 8):
            parts = [C[q, j] * v[j] for j in range(8)]
            while len(parts) > 1:
                parts = [parts[i] + parts[i + 1] for i in range(0, len(parts), 2)]
            M[q] = M[q] - parts[0]
    return outs


def kernel(nz, ny2, basis_ref, stiff_ref, cols_hbm, count_hbm, list_hbm, wt_ref, sum_ref,
           x_ref, s_ref, cols_ref, count_ref, list_ref, xt_ref, cc_ref, pick_ref, acc_ref, gst_ref, sel_ref, ghost_ref,
           halo_out, halo_in, plane_out, plane_in, z_out, z_in, core_out,
           load_sem, halo_sem, plane_sem, z_sem, core_sem, near_sem, far_sem):
    nx = CHIPS_X
    rows = lax.axis_index("rows")
    sub = lax.axis_index("sub")
    z, x = rows // nx, rows % nx
    core = sub % 2
    slabs = nz * nx * ny2
    slab = rows * ny2 + sub
    nplane = nx * ny2
    me_plane = x * ny2 + sub

    def flat(index):
        return (index // ny2, index % ny2)

    prev_id, next_id = flat((slab + slabs - 1) % slabs), flat((slab + 1) % slabs)

    def z_id(index):
        return (index * nx + x, sub)

    barrier = pltpu.get_barrier_semaphore()

    def greet(device):
        pl.semaphore_signal(barrier, inc=1, device_id=device, device_id_type=MESH)

    load_x = pltpu.make_async_copy(basis_ref, x_ref, load_sem.at[0])
    load_s = pltpu.make_async_copy(stiff_ref, s_ref, load_sem.at[1])
    load_c = pltpu.make_async_copy(cols_hbm, cols_ref, load_sem.at[2])
    load_n = pltpu.make_async_copy(count_hbm, count_ref, load_sem.at[3])
    load_l = pltpu.make_async_copy(list_hbm, list_ref, load_sem.at[4])
    load_l.start()
    load_x.start()
    load_c.start()
    load_n.start()
    load_s.start()
    greet(prev_id)
    greet(next_id)
    for q in range(1, ny2):
        greet((rows, (sub + q) % ny2))
    x_peers = [(z * nx + (x + q) % nx, sub) for q in range(1, nx)]
    for peer in x_peers:
        greet(peer)
    greet(z_id((z + 1) % nz))
    greet(z_id((z + nz - 1) % nz))

    load_c.wait()
    load_n.wait()
    cols = cols_ref[...]
    live = iota(cols.shape, 0) < count_ref[...]
    from_prev = jnp.logical_and(cols >= BROWS_DEV, cols < BROWS_DEV + SEND)
    from_next = cols >= BROWS_DEV + SEND
    first = jnp.where(slab == 0, 1, 0)
    last = jnp.where(slab == slabs - 1, 1, 0)
    gone = jnp.where(from_prev, first, 0) + jnp.where(from_next, last, 0)
    cc_ref[...] = jnp.where(jnp.logical_and(live, gone == 0), cols, -1)

    load_l.wait()
    load_x.wait()
    for j in range(BLOCK):
        for t, term in enumerate(split3(x_ref[j])):
            xt_ref[t, LOADS * j : LOADS * (j + 1), :] = term

    place = iota((BROWS_DEV, BROWS_DEV), 0)
    lane = iota((BROWS_DEV, BROWS_DEV), 1)
    lists = jnp.concatenate([list_ref[0:1, :]] * 4 + [list_ref[1:2, :]] * 4, axis=1)
    hit = place == lists
    packed = None
    for q in range(4):
        sel = one_hot(jnp.logical_and(hit, (lane % 128) // SEND == q))
        for t in range(3):
            term = dot(xt_ref[t, 128 * q : 128 * (q + 1), :], sel)
            packed = term if packed is None else packed + term
    halo_out[0] = packed[:, :128]
    halo_out[1] = packed[:, 128:]

    pl.semaphore_wait(barrier, 2 + (ny2 - 1) + (nx - 1) + 2)
    to_prev = pltpu.make_async_remote_copy(
        src_ref=halo_out.at[0], dst_ref=halo_in.at[1], send_sem=halo_sem.at[0],
        recv_sem=halo_sem.at[1], device_id=prev_id, device_id_type=MESH)
    to_next = pltpu.make_async_remote_copy(
        src_ref=halo_out.at[1], dst_ref=halo_in.at[0], send_sem=halo_sem.at[2],
        recv_sem=halo_sem.at[3], device_id=next_id, device_id_type=MESH)
    to_prev.start()
    to_next.start()
    for peer in x_peers:
        pl.semaphore_signal(near_sem, inc=1, device_id=peer, device_id_type=MESH)

    def tell(step):
        for to in ((z + step) % nz, (z + nz - step) % nz):
            pl.semaphore_signal(far_sem.at[step.bit_length() - 1], inc=1, device_id=z_id(to), device_id_type=MESH)

    def hear(step):
        pl.semaphore_wait(far_sem.at[step.bit_length() - 1], 2)

    steps = [1 << e for e in range(8) if 2 * (1 << e) <= nz // 2]
    if steps:
        tell(steps[0])

    def pick_local(k, carry):
        sel = one_hot(place == cc_ref[pl.ds(k, 1), :])
        got = dot(xt_ref[0], sel) + dot(xt_ref[1], sel) + dot(xt_ref[2], sel)
        pick_ref[k] = got.reshape(BLOCK, LOADS, BROWS_DEV)
        return carry

    lax.fori_loop(1, SLOTS, pick_local, 0)
    load_s.wait()
    if len(steps) > 1:
        hear(steps[0])
        tell(steps[1])

    def multiply(k, source, start):
        for c in range(2):
            lanes = slice(128 * c, 128 * (c + 1))
            for h in range(2):
                loads = slice(32 * h, 32 * (h + 1))
                total = None if start else acc_ref[:, loads, lanes]
                for j in range(BLOCK):
                    term = s_ref[k, :, j : j + 1, lanes] * source(j, loads, lanes)[None]
                    total = term if total is None else total + term
                acc_ref[:, loads, lanes] = total

    multiply(0, lambda j, loads, lanes: x_ref[j, loads, lanes], True)

    r = iota((BROWS_DEV, 192), 0)
    n = iota((BROWS_DEV, 192), 1)
    for q in range(4):
        want = (n % 64) // SEND * 128 + SEND * q + n % SEND
        for t in range(3):
            sel_ref[q, t] = one_hot(jnp.logical_and(n // 64 == t, r == want))

    ghost_place = BROWS_DEV + iota((192, BROWS_DEV), 0) % 64

    to_prev.wait_recv()
    to_next.wait_recv()
    sides = [split3(halo_in[0]), split3(halo_in[1])]
    for q in range(4):
        total = None
        for t in range(3):
            term = dot(sides[0][t], sel_ref[q, t, :128]) + dot(sides[1][t], sel_ref[q, t, 128:])
            total = term if total is None else total + term
        gst_ref[128 * q : 128 * (q + 1), :] = total.astype(BF16)

    def add_ghosts(k, carry):
        sel = one_hot(ghost_place == cc_ref[k : k + 1, :])
        got = dot(gst_ref[...], sel).reshape(BLOCK, LOADS, BROWS_DEV)
        pick_ref[k] = pick_ref[k] + got
        return carry

    for k in range(1, SLOTS):
        add_ghosts(k, 0)
    for c in range(2):
        lanes = slice(128 * c, 128 * (c + 1))

        for h in range(LOADS // 16):
            loads = slice(16 * h, 16 * (h + 1))

            def slot(k, total):
                for j in range(BLOCK):
                    total = total + s_ref[k, :, j : j + 1, lanes] * pick_ref[k, j, loads, lanes][None]
                return total

            acc_ref[:, loads, lanes] = lax.fori_loop(1, SLOTS, slot, acc_ref[:, loads, lanes])
        if c == 0 and len(steps) > 2:
            hear(steps[1])
            tell(steps[2])

    gram = None
    for i in range(BLOCK):
        scaled = acc_ref[i] / s_ref[0, i, i : i + 1, :]
        wt_ref[i] = jnp.concatenate(split3(scaled), axis=0)
        term = lax.dot_general(wt_ref[i], wt_ref[i], (((1,), (1,)), ((), ())),
                               preferred_element_type=F32)
        gram = term if gram is None else gram + term
    gram = gram[0:64] + gram[64:128] + gram[128:192]
    gram = gram[:, 0:64] + gram[:, 64:128] + gram[:, 128:192]
    gram = gram * (1.0 / (BLOCK * BROWS_DEV * slabs))

    pack(plane_out, gram)
    pl.semaphore_wait(near_sem, nx - 1)
    plane_in[me_plane] = plane_out[core]

    for dx in (2, 1, 3, 0):
        for dy in range(ny2):
            shift = (ny2 // 2 + dy) % ny2
            if dx or shift:
                to_x, to_sub = (x + dx) % nx, (sub + shift) % ny2
                pltpu.make_async_remote_copy(
                    src_ref=plane_out.at[to_sub % 2], dst_ref=plane_in.at[me_plane],
                    send_sem=plane_sem.at[0], recv_sem=plane_sem.at[1],
                    device_id=(z * nx + to_x, to_sub), device_id_type=MESH).start()

    part = plane_in.at[pl.ds(0, nplane - 1)]
    plane_all = pltpu.make_async_remote_copy(
        src_ref=part, dst_ref=part, send_sem=plane_sem.at[0], recv_sem=plane_sem.at[1],
        device_id=(rows, sub + 1 - 2 * core), device_id_type=MESH)
    plane_all.wait_recv()
    total = jnp.sum(plane_in[...], axis=0)
    z_out[...] = total
    z_in[z] = total

    if steps:
        hear(steps[-1])

    def send_z(q, carry):
        half = (q + 1) // 2
        to = (z + nz // 2 + half * (1 - 2 * (q % 2))) % nz
        pltpu.make_async_remote_copy(
            src_ref=z_out, dst_ref=z_in.at[z], send_sem=z_sem.at[0],
            recv_sem=z_sem.at[1], device_id=z_id(to), device_id_type=MESH).start()
        return carry

    lax.fori_loop(0, nz - 1, send_z, 0)
    part = z_in.at[pl.ds(0, nz - 1)]
    z_all = pltpu.make_async_remote_copy(
        src_ref=part, dst_ref=part, send_sem=z_sem.at[0], recv_sem=z_sem.at[1],
        device_id=z_id((z + 1) % nz), device_id_type=MESH)
    z_all.wait_recv()
    total = jnp.sum(z_in[...], axis=0)
    core_out[...] = total
    sum_ref[core] = total
    to_core = pltpu.make_async_remote_copy(
        src_ref=core_out, dst_ref=sum_ref.at[core], send_sem=core_sem.at[0],
        recv_sem=core_sem.at[1], device_id=(rows, sub + 1 - 2 * core), device_id_type=MESH)
    to_core.start()
    to_core.wait_recv()

    to_prev.wait_send()
    to_next.wait_send()
    plane_all.wait_send()
    z_all.wait_send()
    to_core.wait_send()


def pack(ref, gram):
    wide = [gram[0:16], jnp.concatenate([gram[16:32, 16:64], gram[32:48, 32:48]], axis=1)]
    small = [gram[48:64, 48:64], gram[32:48, 48:64]]
    for c in range(2):
        ref[c, 0:8, :] = jnp.concatenate([wide[c][0:8], wide[c][8:16]], axis=1)
        ref[c, 8:10, :] = jnp.concatenate([small[c][2 * i : 2 * i + 2] for i in range(8)], axis=1)


def unpack(ref):
    wide = [jnp.concatenate([ref[c, 0:8, 0:64], ref[c, 0:8, 64:128]], axis=0) for c in range(2)]
    small = [jnp.concatenate([ref[c, 8:10, 16 * i : 16 * (i + 1)] for i in range(8)], axis=0) for c in range(2)]
    zeros = jnp.zeros((16, 48), F32)
    rows = [
        wide[0],
        jnp.concatenate([zeros[:, 0:16], wide[1][:, 0:48]], axis=1),
        jnp.concatenate([zeros[:, 0:32], wide[1][:, 48:64], small[1]], axis=1),
        jnp.concatenate([zeros, small[0]], axis=1),
    ]
    upper = jnp.concatenate(rows, axis=0)
    keep = iota((LOADS, LOADS), 0) <= iota((LOADS, LOADS), 1)
    return jnp.where(keep, upper, upper.T)


def apply_kernel(wt_ref, sum_ref, out_hbm, factor_hbm, out_ref, factor_ref, rows_ref, cols_ref, near_ref, sems):
    gram = unpack(sum_ref)
    on_diagonal = iota((LOADS, LOADS), 0) == iota((LOADS, LOADS), 1)
    diagonal = jnp.where(on_diagonal, gram, 0.0)
    square = jnp.sum(diagonal, axis=0, keepdims=True)
    lane_scale = lax.rsqrt(square)
    row_scale = lax.rsqrt(jnp.sum(diagonal, axis=1, keepdims=True))
    both = jnp.concatenate([gram * row_scale * lane_scale, jnp.where(on_diagonal, lane_scale, 0.0)], axis=1)
    outs = factor_rows([both[8 * p : 8 * p + 8] for p in range(8)], cols_ref, near_ref)
    for p in range(8):
        for j in range(8):
            rows_ref[8 * p + j : 8 * p + j + 1, :] = outs[p][j][0:1]
    found = rows_ref[...]
    upper = iota((LOADS, LOADS), 0) <= iota((LOADS, LOADS), 1)
    factor_ref[...] = jnp.where(upper, found[:, :LOADS] * (square * lane_scale), 0.0)
    store = pltpu.make_async_copy(factor_ref, factor_hbm, sems.at[BLOCK])
    store.start()
    stores = [store]
    left = jnp.concatenate([jnp.concatenate([term] * 3, axis=1) for term in split3(found[:, LOADS:])], axis=0)
    for i in range(BLOCK):
        got = dot(left, wt_ref[i])
        out_ref[i] = got[0:64] + got[64:128] + got[128:192]
        store = pltpu.make_async_copy(out_ref.at[i], out_hbm.at[i], sems.at[i])
        store.start()
        stores.append(store)
    for store in stores:
        store.wait()


def on_device(nz, ny2, basis, stiffness, col_index, block_count, send_list):
    nplane = CHIPS_X * ny2
    vmem = pl.BlockSpec(memory_space=pltpu.VMEM)
    hbm = pl.BlockSpec(memory_space=pltpu.MemorySpace.HBM)
    held = [
        pltpu.with_memory_space_constraint(value, pltpu.MemorySpace.HBM)
        for value in (basis, stiffness, col_index, block_count.reshape(1, BROWS_DEV), send_list)
    ]
    wt, total = pl.pallas_call(
        functools.partial(kernel, nz, ny2),
        out_shape=(
            jax.ShapeDtypeStruct((BLOCK, 3 * LOADS, BROWS_DEV), BF16),
            jax.ShapeDtypeStruct((2, 10, 128), F32),
        ),
        in_specs=[hbm, hbm, hbm, hbm, hbm],
        out_specs=(vmem, vmem),
        scratch_shapes=[
            pltpu.VMEM((BLOCK, LOADS, BROWS_DEV), F32),
            pltpu.VMEM((SLOTS, BLOCK, BLOCK, BROWS_DEV), F32),
            pltpu.VMEM((SLOTS, BROWS_DEV), jnp.int32),
            pltpu.VMEM((1, BROWS_DEV), jnp.int32),
            pltpu.VMEM((2, SEND), jnp.int32),
            pltpu.VMEM((3, BLOCK * LOADS, BROWS_DEV), BF16),
            pltpu.VMEM((SLOTS, BROWS_DEV), jnp.int32),
            pltpu.VMEM((SLOTS, BLOCK, LOADS, BROWS_DEV), F32),
            pltpu.VMEM((BLOCK, LOADS, BROWS_DEV), F32),
            pltpu.VMEM((BLOCK * LOADS, 192), BF16),
            pltpu.VMEM((4, 3, BROWS_DEV, 192), BF16),
            pltpu.VMEM((SLOTS, 192, BROWS_DEV), BF16),
            pltpu.VMEM((2, 128, 128), F32),
            pltpu.VMEM((2, 128, 128), F32),
            pltpu.VMEM((2, 10, 128), F32),
            pltpu.VMEM((nplane, 10, 128), F32),
            pltpu.VMEM((10, 128), F32),
            pltpu.VMEM((nz, 10, 128), F32),
            pltpu.VMEM((10, 128), F32),
            pltpu.SemaphoreType.DMA((5,)),
            pltpu.SemaphoreType.DMA((4,)),
            pltpu.SemaphoreType.DMA((2,)),
            pltpu.SemaphoreType.DMA((2,)),
            pltpu.SemaphoreType.DMA((2,)),
            pltpu.SemaphoreType.REGULAR,
            pltpu.SemaphoreType.REGULAR((4,)),
        ],
        name="arnoldi_step",
        compiler_params=pltpu.CompilerParams(
            collective_id=1, has_side_effects=True, vmem_limit_bytes=40 * 1024 * 1024),
    )(*held)
    return pl.pallas_call(
        apply_kernel,
        out_shape=(jax.ShapeDtypeStruct(basis.shape, F32), jax.ShapeDtypeStruct((LOADS, LOADS), F32)),
        in_specs=[vmem, vmem],
        out_specs=(hbm, hbm),
        scratch_shapes=[
            pltpu.VMEM((BLOCK, LOADS, BROWS_DEV), F32),
            pltpu.VMEM((LOADS, LOADS), F32),
            pltpu.VMEM((LOADS, 128), F32),
            pltpu.VMEM((8, 9, 8, 128), F32),
            pltpu.VMEM((8, 8, 8, 128), F32),
            pltpu.SemaphoreType.DMA((BLOCK + 1,)),
        ],
        name="apply",
        compiler_params=pltpu.CompilerParams(vmem_limit_bytes=16 * 1024 * 1024),
    )(wt, total)


def solution(mesh):
    nz, ny2 = mesh.shape["rows"] // CHIPS_X, mesh.shape["sub"]
    in_specs = (
        P(None, None, ("rows", "sub")),
        P(None, None, None, ("rows", "sub")),
        P(None, ("rows", "sub")),
        P(("rows", "sub")),
        P(None, ("rows", "sub")),
    )
    out_specs = (P(None, None, ("rows", "sub")), P())
    return jax.shard_map(
        functools.partial(on_device, nz, ny2), mesh=mesh, in_specs=in_specs, out_specs=out_specs,
        check_vma=False,
    )
```

```python
import functools

import jax
import jax.numpy as jnp
from jax import lax
from jax.experimental import pallas as pl
from jax.experimental.pallas import tpu as pltpu
from jax.sharding import PartitionSpec as P

BLOCK = 8
LOADS = 64
SLOTS = 12
BROWS_DEV = 256
SEND = 32
CHIPS_X = 4
F32 = jnp.float32
BF16 = jnp.bfloat16
MESH = pl.DeviceIdType.MESH


def split3(value):
    high = value.astype(BF16)
    rest = value - high.astype(F32)
    mid = rest.astype(BF16)
    low = (rest - mid.astype(F32)).astype(BF16)
    return high, mid, low


def dot(a, b):
    return lax.dot_general(a, b, (((1,), (0,)), ((), ())), preferred_element_type=F32)


def one_hot(condition):
    return jnp.where(condition, 1.0, 0.0).astype(BF16)


def iota(shape, dim):
    return lax.broadcasted_iota(jnp.int32, shape, dim)


def factor_rows(M, cols_ref, near_ref):
    M = list(M)
    outs = []
    full = (8, 128)
    for p in range(8):
        T = M[p]
        cols_ref[p, 8] = T
        C = {}
        for q in range(p + 1, 8):
            for j in range(8):
                C[q, j] = jnp.broadcast_to(M[q][:, 8 * p + j : 8 * p + j + 1], full)
        if p == 0:
            corner = [jnp.broadcast_to(T[:, j : j + 1], full) for j in range(8)]
        for j in range(8):
            cols_ref[p, j] = corner[j]
        if p < 7:
            corner = [jnp.broadcast_to(M[p + 1][:, 8 * p + 8 + j : 8 * p + 9 + j], full) for j in range(8)]
        t = [jnp.broadcast_to(cols_ref[p, 8, r : r + 1, :], full) for r in range(8)]
        s = {}
        for r in range(8):
            for m in range(r, 8):
                s[r, m] = jnp.broadcast_to(cols_ref[p, m, r : r + 1, :], full)
        inv, f, u = [None] * 8, {}, [None] * 8
        near = [C[p + 1, j] for j in range(8)] if p < 7 else None
        for j in range(0, 8, 2):
            a, b = s[j, j], s[j, j + 1]
            first = lax.rsqrt(a)
            both = lax.rsqrt(a * s[j + 1, j + 1] - b * b)
            second = first * both
            inv[j], inv[j + 1] = first, a * first * both
            f[j, j + 1] = b * first
            for m in range(j + 2, 8):
                f[j, m] = s[j, m] * first
                f[j + 1, m] = (a * s[j + 1, m] - b * s[j, m]) * second
            u[j], u[j + 1] = t[j] * first, (a * t[j + 1] - b * t[j]) * second
            for m in range(j + 2, 8):
                for n in range(m, 8):
                    s[m, n] = s[m, n] - f[j, m] * f[j, n] - f[j + 1, m] * f[j + 1, n]
                t[m] = t[m] - f[j, m] * u[j] - f[j + 1, m] * u[j + 1]
            if near:
                e0, e1 = near[j] * first, (a * near[j + 1] - b * near[j]) * second
                for m in range(j + 2, 8):
                    near[m] = near[m] - f[j, m] * e0 - f[j + 1, m] * e1
                M[p + 1] = M[p + 1] - e0 * u[j] - e1 * u[j + 1]
                near_ref[p, j] = e0
                near_ref[p, j + 1] = e1
                for m in range(8):
                    d0 = jnp.broadcast_to(near_ref[p, j, m : m + 1, :], full)
                    d1 = jnp.broadcast_to(near_ref[p, j + 1, m : m + 1, :], full)
                    corner[m] = corner[m] - e0 * d0 - e1 * d1
        outs.append(u)
        if p >= 6:
            continue
        v = [None] * 8
        for j in range(7, -1, -1):
            a = u[j]
            for m in range(j + 1, 8):
                a = a - f[j, m] * v[m]
            v[j] = a * inv[j]
        for q in range(p + 2, 8):
            parts = [C[q, j] * v[j] for j in range(8)]
            while len(parts) > 1:
                parts = [parts[i] + parts[i + 1] for i in range(0, len(parts), 2)]
            M[q] = M[q] - parts[0]
    return outs


def kernel(nz, ny2, basis_ref, stiff_ref, cols_hbm, count_hbm, list_hbm, wt_ref, sum_ref,
           x_ref, s_ref, cols_ref, count_ref, list_ref, xt_ref, cc_ref, pick_ref, acc_ref, gst_ref, sel_ref, ghost_ref,
           halo_out, halo_in, plane_out, plane_in, z_out, z_in, core_out, direct_in,
           load_sem, halo_sem, plane_sem, z_sem, core_sem, near_sem, far_sem, direct_sem):
    nx = CHIPS_X
    rows = lax.axis_index("rows")
    sub = lax.axis_index("sub")
    z, x = rows // nx, rows % nx
    core = sub % 2
    slabs = nz * nx * ny2
    slab = rows * ny2 + sub
    nplane = nx * ny2
    me_plane = x * ny2 + sub

    def flat(index):
        return (index // ny2, index % ny2)

    prev_id, next_id = flat((slab + slabs - 1) % slabs), flat((slab + 1) % slabs)

    def z_id(index):
        return (index * nx + x, sub)

    barrier = pltpu.get_barrier_semaphore()

    def greet(device):
        pl.semaphore_signal(barrier, inc=1, device_id=device, device_id_type=MESH)

    load_x = pltpu.make_async_copy(basis_ref, x_ref, load_sem.at[0])
    load_s = pltpu.make_async_copy(stiff_ref, s_ref, load_sem.at[1])
    load_c = pltpu.make_async_copy(cols_hbm, cols_ref, load_sem.at[2])
    load_n = pltpu.make_async_copy(count_hbm, count_ref, load_sem.at[3])
    load_l = pltpu.make_async_copy(list_hbm, list_ref, load_sem.at[4])
    load_l.start()
    load_x.start()
    load_c.start()
    load_n.start()
    load_s.start()
    greet(prev_id)
    greet(next_id)
    for q in range(1, ny2):
        greet((rows, (sub + q) % ny2))
    x_peers = [(z * nx + (x + q) % nx, sub) for q in range(1, nx)]
    for peer in x_peers:
        greet(peer)
    greet(z_id((z + 1) % nz))
    greet(z_id((z + nz - 1) % nz))

    is_first = jnp.logical_and(rows == 0, sub == 1)

    @pl.when(is_first)
    def _():
        greet((nx, 0))
        greet(((nz - 1) * nx, 0))

    is_source = jnp.logical_and(x == 0, sub == 0)
    extra = jnp.where(jnp.logical_and(is_source, z == 1), 1, 0)
    extra = extra + jnp.where(jnp.logical_and(is_source, z == nz - 1), 1, 0)

    load_c.wait()
    load_n.wait()
    cols = cols_ref[...]
    live = iota(cols.shape, 0) < count_ref[...]
    from_prev = jnp.logical_and(cols >= BROWS_DEV, cols < BROWS_DEV + SEND)
    from_next = cols >= BROWS_DEV + SEND
    first = jnp.where(slab == 0, 1, 0)
    last = jnp.where(slab == slabs - 1, 1, 0)
    gone = jnp.where(from_prev, first, 0) + jnp.where(from_next, last, 0)
    cc_ref[...] = jnp.where(jnp.logical_and(live, gone == 0), cols, -1)

    load_l.wait()
    load_x.wait()
    for j in range(BLOCK):
        for t, term in enumerate(split3(x_ref[j])):
            xt_ref[t, LOADS * j : LOADS * (j + 1), :] = term

    place = iota((BROWS_DEV, BROWS_DEV), 0)
    lane = iota((BROWS_DEV, BROWS_DEV), 1)
    lists = jnp.concatenate([list_ref[0:1, :]] * 4 + [list_ref[1:2, :]] * 4, axis=1)
    hit = place == lists
    packed = None
    for q in range(4):
        sel = one_hot(jnp.logical_and(hit, (lane % 128) // SEND == q))
        for t in range(3):
            term = dot(xt_ref[t, 128 * q : 128 * (q + 1), :], sel)
            packed = term if packed is None else packed + term
    halo_out[0] = packed[:, :128]
    halo_out[1] = packed[:, 128:]

    pl.semaphore_wait(barrier, 2 + (ny2 - 1) + (nx - 1) + 2 + extra)
    to_prev = pltpu.make_async_remote_copy(
        src_ref=halo_out.at[0], dst_ref=halo_in.at[1], send_sem=halo_sem.at[0],
        recv_sem=halo_sem.at[1], device_id=prev_id, device_id_type=MESH)
    to_next = pltpu.make_async_remote_copy(
        src_ref=halo_out.at[1], dst_ref=halo_in.at[0], send_sem=halo_sem.at[2],
        recv_sem=halo_sem.at[3], device_id=next_id, device_id_type=MESH)
    to_prev.start()
    to_next.start()
    for peer in x_peers:
        pl.semaphore_signal(near_sem, inc=1, device_id=peer, device_id_type=MESH)

    def tell(step):
        for to in ((z + step) % nz, (z + nz - step) % nz):
            pl.semaphore_signal(far_sem.at[step.bit_length() - 1], inc=1, device_id=z_id(to), device_id_type=MESH)

    def hear(step):
        pl.semaphore_wait(far_sem.at[step.bit_length() - 1], 2)

    steps = [1 << e for e in range(8) if 2 * (1 << e) <= nz // 2]
    if steps:
        tell(steps[0])

    def pick_local(k, carry):
        sel = one_hot(place == cc_ref[pl.ds(k, 1), :])
        got = dot(xt_ref[0], sel) + dot(xt_ref[1], sel) + dot(xt_ref[2], sel)
        pick_ref[k] = got.reshape(BLOCK, LOADS, BROWS_DEV)
        return carry

    lax.fori_loop(1, SLOTS, pick_local, 0)
    load_s.wait()
    if len(steps) > 1:
        hear(steps[0])
        tell(steps[1])

    def multiply(k, source, start):
        for c in range(2):
            lanes = slice(128 * c, 128 * (c + 1))
            for h in range(2):
                loads = slice(32 * h, 32 * (h + 1))
                total = None if start else acc_ref[:, loads, lanes]
                for j in range(BLOCK):
                    term = s_ref[k, :, j : j + 1, lanes] * source(j, loads, lanes)[None]
                    total = term if total is None else total + term
                acc_ref[:, loads, lanes] = total

    multiply(0, lambda j, loads, lanes: x_ref[j, loads, lanes], True)

    r = iota((BROWS_DEV, 192), 0)
    n = iota((BROWS_DEV, 192), 1)
    for q in range(4):
        want = (n % 64) // SEND * 128 + SEND * q + n % SEND
        for t in range(3):
            sel_ref[q, t] = one_hot(jnp.logical_and(n // 64 == t, r == want))

    ghost_place = BROWS_DEV + iota((192, BROWS_DEV), 0) % 64

    to_prev.wait_recv()
    to_next.wait_recv()
    sides = [split3(halo_in[0]), split3(halo_in[1])]
    for q in range(4):
        total = None
        for t in range(3):
            term = dot(sides[0][t], sel_ref[q, t, :128]) + dot(sides[1][t], sel_ref[q, t, 128:])
            total = term if total is None else total + term
        gst_ref[128 * q : 128 * (q + 1), :] = total.astype(BF16)

    def add_ghosts(k, carry):
        sel = one_hot(ghost_place == cc_ref[k : k + 1, :])
        got = dot(gst_ref[...], sel).reshape(BLOCK, LOADS, BROWS_DEV)
        pick_ref[k] = pick_ref[k] + got
        return carry

    for k in range(1, SLOTS):
        add_ghosts(k, 0)
    for c in range(2):
        lanes = slice(128 * c, 128 * (c + 1))

        for h in range(LOADS // 16):
            loads = slice(16 * h, 16 * (h + 1))

            def slot(k, total):
                for j in range(BLOCK):
                    total = total + s_ref[k, :, j : j + 1, lanes] * pick_ref[k, j, loads, lanes][None]
                return total

            acc_ref[:, loads, lanes] = lax.fori_loop(1, SLOTS, slot, acc_ref[:, loads, lanes])
        if c == 0 and len(steps) > 2:
            hear(steps[1])
            tell(steps[2])

    gram = None
    for i in range(BLOCK):
        scaled = acc_ref[i] / s_ref[0, i, i : i + 1, :]
        wt_ref[i] = jnp.concatenate(split3(scaled), axis=0)
        term = lax.dot_general(wt_ref[i], wt_ref[i], (((1,), (1,)), ((), ())),
                               preferred_element_type=F32)
        gram = term if gram is None else gram + term
    gram = gram[0:64] + gram[64:128] + gram[128:192]
    gram = gram[:, 0:64] + gram[:, 64:128] + gram[:, 128:192]
    gram = gram * (1.0 / (BLOCK * BROWS_DEV * slabs))

    pack(plane_out, gram)
    pl.semaphore_wait(near_sem, nx - 1)
    plane_in[me_plane] = plane_out[core]

    for dx in (2, 1, 3, 0):
        for dy in range(ny2):
            shift = (ny2 // 2 + dy) % ny2
            if dx or shift:
                to_x, to_sub = (x + dx) % nx, (sub + shift) % ny2
                pltpu.make_async_remote_copy(
                    src_ref=plane_out.at[to_sub % 2], dst_ref=plane_in.at[me_plane],
                    send_sem=plane_sem.at[0], recv_sem=plane_sem.at[1],
                    device_id=(z * nx + to_x, to_sub), device_id_type=MESH).start()

    part = plane_in.at[pl.ds(0, nplane - 1)]
    plane_all = pltpu.make_async_remote_copy(
        src_ref=part, dst_ref=part, send_sem=plane_sem.at[0], recv_sem=plane_sem.at[1],
        device_id=(rows, sub + 1 - 2 * core), device_id_type=MESH)
    plane_all.wait_recv()
    total = jnp.sum(plane_in[...], axis=0)
    z_out[...] = total
    z_in[z] = total

    if steps:
        hear(steps[-1])

    is_mate = jnp.logical_and(rows == 0, sub == 0)
    direct = pltpu.make_async_remote_copy(
        src_ref=z_out, dst_ref=direct_in.at[z], send_sem=direct_sem.at[0], recv_sem=direct_sem.at[1],
        device_id=(0, 1), device_id_type=MESH)

    @pl.when(is_source)
    def _():
        direct.start()

    def send_z(q, carry):
        half = (q + 1) // 2
        to = (z + nz // 2 + half * (1 - 2 * (q % 2))) % nz
        pltpu.make_async_remote_copy(
            src_ref=z_out, dst_ref=z_in.at[z], send_sem=z_sem.at[0],
            recv_sem=z_sem.at[1], device_id=z_id(to), device_id_type=MESH).start()
        return carry

    lax.fori_loop(0, nz - 1, send_z, 0)
    part = z_in.at[pl.ds(0, nz - 1)]
    z_all = pltpu.make_async_remote_copy(
        src_ref=part, dst_ref=part, send_sem=z_sem.at[0], recv_sem=z_sem.at[1],
        device_id=z_id((z + 1) % nz), device_id_type=MESH)
    z_all.wait_recv()
    total = jnp.sum(z_in[...], axis=0)
    core_out[...] = total
    sum_ref[core] = total
    to_core = pltpu.make_async_remote_copy(
        src_ref=core_out, dst_ref=sum_ref.at[core], send_sem=core_sem.at[0],
        recv_sem=core_sem.at[1], device_id=(rows, sub + 1 - 2 * core), device_id_type=MESH)

    @pl.when(jnp.logical_not(is_mate))
    def _():
        to_core.start()

    @pl.when(jnp.logical_not(is_first))
    def _():
        to_core.wait_recv()

    @pl.when(is_first)
    def _():
        pltpu.make_async_remote_copy(
            src_ref=direct_in, dst_ref=direct_in, send_sem=direct_sem.at[0], recv_sem=direct_sem.at[1],
            device_id=(0, 0), device_id_type=MESH).wait_recv()
        sum_ref[0] = jnp.sum(direct_in[...], axis=0)


    to_prev.wait_send()
    to_next.wait_send()
    plane_all.wait_send()
    z_all.wait_send()

    @pl.when(is_source)
    def _():
        direct.wait_send()

    @pl.when(jnp.logical_not(is_mate))
    def _():
        to_core.wait_send()


def pack(ref, gram):
    wide = [gram[0:16], jnp.concatenate([gram[16:32, 16:64], gram[32:48, 32:48]], axis=1)]
    small = [gram[48:64, 48:64], gram[32:48, 48:64]]
    for c in range(2):
        ref[c, 0:8, :] = jnp.concatenate([wide[c][0:8], wide[c][8:16]], axis=1)
        ref[c, 8:10, :] = jnp.concatenate([small[c][2 * i : 2 * i + 2] for i in range(8)], axis=1)


def unpack(ref):
    wide = [jnp.concatenate([ref[c, 0:8, 0:64], ref[c, 0:8, 64:128]], axis=0) for c in range(2)]
    small = [jnp.concatenate([ref[c, 8:10, 16 * i : 16 * (i + 1)] for i in range(8)], axis=0) for c in range(2)]
    zeros = jnp.zeros((16, 48), F32)
    rows = [
        wide[0],
        jnp.concatenate([zeros[:, 0:16], wide[1][:, 0:48]], axis=1),
        jnp.concatenate([zeros[:, 0:32], wide[1][:, 48:64], small[1]], axis=1),
        jnp.concatenate([zeros, small[0]], axis=1),
    ]
    upper = jnp.concatenate(rows, axis=0)
    keep = iota((LOADS, LOADS), 0) <= iota((LOADS, LOADS), 1)
    return jnp.where(keep, upper, upper.T)


def apply_kernel(wt_ref, sum_ref, out_hbm, factor_hbm, out_ref, factor_ref, rows_ref, cols_ref, near_ref, sems):
    gram = unpack(sum_ref)
    on_diagonal = iota((LOADS, LOADS), 0) == iota((LOADS, LOADS), 1)
    diagonal = jnp.where(on_diagonal, gram, 0.0)
    square = jnp.sum(diagonal, axis=0, keepdims=True)
    lane_scale = lax.rsqrt(square)
    row_scale = lax.rsqrt(jnp.sum(diagonal, axis=1, keepdims=True))
    both = jnp.concatenate([gram * row_scale * lane_scale, jnp.where(on_diagonal, lane_scale, 0.0)], axis=1)
    outs = factor_rows([both[8 * p : 8 * p + 8] for p in range(8)], cols_ref, near_ref)
    for p in range(8):
        for j in range(8):
            rows_ref[8 * p + j : 8 * p + j + 1, :] = outs[p][j][0:1]
    found = rows_ref[...]
    upper = iota((LOADS, LOADS), 0) <= iota((LOADS, LOADS), 1)
    factor_ref[...] = jnp.where(upper, found[:, :LOADS] * (square * lane_scale), 0.0)
    store = pltpu.make_async_copy(factor_ref, factor_hbm, sems.at[BLOCK])
    store.start()
    stores = [store]
    left = jnp.concatenate([jnp.concatenate([term] * 3, axis=1) for term in split3(found[:, LOADS:])], axis=0)
    for i in range(BLOCK):
        got = dot(left, wt_ref[i])
        out_ref[i] = got[0:64] + got[64:128] + got[128:192]
        store = pltpu.make_async_copy(out_ref.at[i], out_hbm.at[i], sems.at[i])
        store.start()
        stores.append(store)
    for store in stores:
        store.wait()


def on_device(nz, ny2, basis, stiffness, col_index, block_count, send_list):
    nplane = CHIPS_X * ny2
    vmem = pl.BlockSpec(memory_space=pltpu.VMEM)
    hbm = pl.BlockSpec(memory_space=pltpu.MemorySpace.HBM)
    held = [
        pltpu.with_memory_space_constraint(value, pltpu.MemorySpace.HBM)
        for value in (basis, stiffness, col_index, block_count.reshape(1, BROWS_DEV), send_list)
    ]
    wt, total = pl.pallas_call(
        functools.partial(kernel, nz, ny2),
        out_shape=(
            jax.ShapeDtypeStruct((BLOCK, 3 * LOADS, BROWS_DEV), BF16),
            jax.ShapeDtypeStruct((2, 10, 128), F32),
        ),
        in_specs=[hbm, hbm, hbm, hbm, hbm],
        out_specs=(vmem, vmem),
        scratch_shapes=[
            pltpu.VMEM((BLOCK, LOADS, BROWS_DEV), F32),
            pltpu.VMEM((SLOTS, BLOCK, BLOCK, BROWS_DEV), F32),
            pltpu.VMEM((SLOTS, BROWS_DEV), jnp.int32),
            pltpu.VMEM((1, BROWS_DEV), jnp.int32),
            pltpu.VMEM((2, SEND), jnp.int32),
            pltpu.VMEM((3, BLOCK * LOADS, BROWS_DEV), BF16),
            pltpu.VMEM((SLOTS, BROWS_DEV), jnp.int32),
            pltpu.VMEM((SLOTS, BLOCK, LOADS, BROWS_DEV), F32),
            pltpu.VMEM((BLOCK, LOADS, BROWS_DEV), F32),
            pltpu.VMEM((BLOCK * LOADS, 192), BF16),
            pltpu.VMEM((4, 3, BROWS_DEV, 192), BF16),
            pltpu.VMEM((SLOTS, 192, BROWS_DEV), BF16),
            pltpu.VMEM((2, 128, 128), F32),
            pltpu.VMEM((2, 128, 128), F32),
            pltpu.VMEM((2, 10, 128), F32),
            pltpu.VMEM((nplane, 10, 128), F32),
            pltpu.VMEM((10, 128), F32),
            pltpu.VMEM((nz, 10, 128), F32),
            pltpu.VMEM((10, 128), F32),
            pltpu.VMEM((nz, 10, 128), F32),
            pltpu.SemaphoreType.DMA((5,)),
            pltpu.SemaphoreType.DMA((4,)),
            pltpu.SemaphoreType.DMA((2,)),
            pltpu.SemaphoreType.DMA((2,)),
            pltpu.SemaphoreType.DMA((2,)),
            pltpu.SemaphoreType.REGULAR,
            pltpu.SemaphoreType.REGULAR((4,)),
            pltpu.SemaphoreType.DMA((2,)),
        ],
        name="arnoldi_step",
        compiler_params=pltpu.CompilerParams(
            collective_id=1, has_side_effects=True, vmem_limit_bytes=40 * 1024 * 1024),
    )(*held)
    return pl.pallas_call(
        apply_kernel,
        out_shape=(jax.ShapeDtypeStruct(basis.shape, F32), jax.ShapeDtypeStruct((LOADS, LOADS), F32)),
        in_specs=[vmem, vmem],
        out_specs=(hbm, hbm),
        scratch_shapes=[
            pltpu.VMEM((BLOCK, LOADS, BROWS_DEV), F32),
            pltpu.VMEM((LOADS, LOADS), F32),
            pltpu.VMEM((LOADS, 128), F32),
            pltpu.VMEM((8, 9, 8, 128), F32),
            pltpu.VMEM((8, 8, 8, 128), F32),
            pltpu.SemaphoreType.DMA((BLOCK + 1,)),
        ],
        name="apply",
        compiler_params=pltpu.CompilerParams(vmem_limit_bytes=16 * 1024 * 1024),
    )(wt, total)


def solution(mesh):
    nz, ny2 = mesh.shape["rows"] // CHIPS_X, mesh.shape["sub"]
    in_specs = (
        P(None, None, ("rows", "sub")),
        P(None, None, None, ("rows", "sub")),
        P(None, ("rows", "sub")),
        P(("rows", "sub")),
        P(None, ("rows", "sub")),
    )
    out_specs = (P(None, None, ("rows", "sub")), P())
    return jax.shard_map(
        functools.partial(on_device, nz, ny2), mesh=mesh, in_specs=in_specs, out_specs=out_specs,
        check_vma=False,
    )
```

```python
import functools

import jax
import jax.numpy as jnp
from jax import lax
from jax.experimental import pallas as pl
from jax.experimental.pallas import tpu as pltpu
from jax.sharding import PartitionSpec as P

BLOCK = 8
LOADS = 64
SLOTS = 12
BROWS_DEV = 256
SEND = 32
CHIPS_X = 4
F32 = jnp.float32
BF16 = jnp.bfloat16
MESH = pl.DeviceIdType.MESH


def split3(value):
    high = value.astype(BF16)
    rest = value - high.astype(F32)
    mid = rest.astype(BF16)
    low = (rest - mid.astype(F32)).astype(BF16)
    return high, mid, low


def dot(a, b):
    return lax.dot_general(a, b, (((1,), (0,)), ((), ())), preferred_element_type=F32)


def one_hot(condition):
    return jnp.where(condition, 1.0, 0.0).astype(BF16)


def iota(shape, dim):
    return lax.broadcasted_iota(jnp.int32, shape, dim)


def factor_rows(M, cols_ref, near_ref):
    M = list(M)
    outs = []
    full = (8, 128)
    for p in range(8):
        T = M[p]
        cols_ref[p, 8] = T
        C = {}
        for q in range(p + 1, 8):
            for j in range(8):
                C[q, j] = jnp.broadcast_to(M[q][:, 8 * p + j : 8 * p + j + 1], full)
        if p == 0:
            corner = [jnp.broadcast_to(T[:, j : j + 1], full) for j in range(8)]
        for j in range(8):
            cols_ref[p, j] = corner[j]
        if p < 7:
            corner = [jnp.broadcast_to(M[p + 1][:, 8 * p + 8 + j : 8 * p + 9 + j], full) for j in range(8)]
        t = [jnp.broadcast_to(cols_ref[p, 8, r : r + 1, :], full) for r in range(8)]
        s = {}
        for r in range(8):
            for m in range(r, 8):
                s[r, m] = jnp.broadcast_to(cols_ref[p, m, r : r + 1, :], full)
        inv, f, u = [None] * 8, {}, [None] * 8
        near = [C[p + 1, j] for j in range(8)] if p < 7 else None
        for j in range(0, 8, 2):
            a, b = s[j, j], s[j, j + 1]
            first = lax.rsqrt(a)
            both = lax.rsqrt(a * s[j + 1, j + 1] - b * b)
            second = first * both
            inv[j], inv[j + 1] = first, a * first * both
            f[j, j + 1] = b * first
            for m in range(j + 2, 8):
                f[j, m] = s[j, m] * first
                f[j + 1, m] = (a * s[j + 1, m] - b * s[j, m]) * second
            u[j], u[j + 1] = t[j] * first, (a * t[j + 1] - b * t[j]) * second
            for m in range(j + 2, 8):
                for n in range(m, 8):
                    s[m, n] = s[m, n] - f[j, m] * f[j, n] - f[j + 1, m] * f[j + 1, n]
                t[m] = t[m] - f[j, m] * u[j] - f[j + 1, m] * u[j + 1]
            if near:
                e0, e1 = near[j] * first, (a * near[j + 1] - b * near[j]) * second
                for m in range(j + 2, 8):
                    near[m] = near[m] - f[j, m] * e0 - f[j + 1, m] * e1
                M[p + 1] = M[p + 1] - e0 * u[j] - e1 * u[j + 1]
                near_ref[p, j] = e0
                near_ref[p, j + 1] = e1
                for m in range(8):
                    d0 = jnp.broadcast_to(near_ref[p, j, m : m + 1, :], full)
                    d1 = jnp.broadcast_to(near_ref[p, j + 1, m : m + 1, :], full)
                    corner[m] = corner[m] - e0 * d0 - e1 * d1
        outs.append(u)
        if p >= 6:
            continue
        v = [None] * 8
        for j in range(7, -1, -1):
            a = u[j]
            for m in range(j + 1, 8):
                a = a - f[j, m] * v[m]
            v[j] = a * inv[j]
        for q in range(p + 2, 8):
            parts = [C[q, j] * v[j] for j in range(8)]
            while len(parts) > 1:
                parts = [parts[i] + parts[i + 1] for i in range(0, len(parts), 2)]
            M[q] = M[q] - parts[0]
    return outs


def kernel(nz, ny2, basis_ref, stiff_ref, cols_hbm, count_hbm, list_hbm, wt_ref, sum_ref,
           x_ref, s_ref, cols_ref, count_ref, list_ref, xt_ref, cc_ref, pick_ref, acc_ref, gst_ref, sel_ref, ghost_ref,
           halo_out, halo_in, plane_out, plane_in, z_out, z_in, core_out, direct_in,
           load_sem, halo_sem, plane_sem, z_sem, core_sem, near_sem, far_sem, direct_sem):
    nx = CHIPS_X
    rows = lax.axis_index("rows")
    sub = lax.axis_index("sub")
    z, x = rows // nx, rows % nx
    core = sub % 2
    slabs = nz * nx * ny2
    slab = rows * ny2 + sub
    nplane = nx * ny2
    me_plane = x * ny2 + sub

    def flat(index):
        return (index // ny2, index % ny2)

    prev_id, next_id = flat((slab + slabs - 1) % slabs), flat((slab + 1) % slabs)

    def z_id(index):
        return (index * nx + x, sub)

    barrier = pltpu.get_barrier_semaphore()

    def greet(device):
        pl.semaphore_signal(barrier, inc=1, device_id=device, device_id_type=MESH)

    load_x = pltpu.make_async_copy(basis_ref, x_ref, load_sem.at[0])
    load_s = pltpu.make_async_copy(stiff_ref, s_ref, load_sem.at[1])
    load_c = pltpu.make_async_copy(cols_hbm, cols_ref, load_sem.at[2])
    load_n = pltpu.make_async_copy(count_hbm, count_ref, load_sem.at[3])
    load_l = pltpu.make_async_copy(list_hbm, list_ref, load_sem.at[4])
    load_l.start()
    load_x.start()
    load_c.start()
    load_n.start()
    load_s.start()
    greet(prev_id)
    greet(next_id)
    for q in range(1, ny2):
        greet((rows, (sub + q) % ny2))
    x_peers = [(z * nx + (x + q) % nx, sub) for q in range(1, nx)]
    for peer in x_peers:
        greet(peer)
    greet(z_id((z + 1) % nz))
    greet(z_id((z + nz - 1) % nz))

    is_first = jnp.logical_and(rows == 0, sub == 1)

    @pl.when(is_first)
    def _():
        greet((nx, 0))
        greet(((nz - 1) * nx, 0))

    is_source = jnp.logical_and(x == 0, sub == 0)
    extra = jnp.where(jnp.logical_and(is_source, z == 1), 1, 0)
    extra = extra + jnp.where(jnp.logical_and(is_source, z == nz - 1), 1, 0)

    load_c.wait()
    load_n.wait()
    cols = cols_ref[...]
    live = iota(cols.shape, 0) < count_ref[...]
    from_prev = jnp.logical_and(cols >= BROWS_DEV, cols < BROWS_DEV + SEND)
    from_next = cols >= BROWS_DEV + SEND
    first = jnp.where(slab == 0, 1, 0)
    last = jnp.where(slab == slabs - 1, 1, 0)
    gone = jnp.where(from_prev, first, 0) + jnp.where(from_next, last, 0)
    cc_ref[...] = jnp.where(jnp.logical_and(live, gone == 0), cols, -1)

    load_l.wait()
    load_x.wait()
    for j in range(BLOCK):
        for t, term in enumerate(split3(x_ref[j])):
            xt_ref[t, LOADS * j : LOADS * (j + 1), :] = term

    place = iota((BROWS_DEV, BROWS_DEV), 0)
    lane = iota((BROWS_DEV, BROWS_DEV), 1)
    lists = jnp.concatenate([list_ref[0:1, :]] * 4 + [list_ref[1:2, :]] * 4, axis=1)
    hit = place == lists
    packed = None
    for q in range(4):
        sel = one_hot(jnp.logical_and(hit, (lane % 128) // SEND == q))
        for t in range(3):
            term = dot(xt_ref[t, 128 * q : 128 * (q + 1), :], sel)
            packed = term if packed is None else packed + term
    halo_out[0] = packed[:, :128]
    halo_out[1] = packed[:, 128:]

    pl.semaphore_wait(barrier, 2 + (ny2 - 1) + (nx - 1) + 2 + extra)
    to_prev = pltpu.make_async_remote_copy(
        src_ref=halo_out.at[0], dst_ref=halo_in.at[1], send_sem=halo_sem.at[0],
        recv_sem=halo_sem.at[1], device_id=prev_id, device_id_type=MESH)
    to_next = pltpu.make_async_remote_copy(
        src_ref=halo_out.at[1], dst_ref=halo_in.at[0], send_sem=halo_sem.at[2],
        recv_sem=halo_sem.at[3], device_id=next_id, device_id_type=MESH)
    to_prev.start()
    to_next.start()
    for peer in x_peers:
        pl.semaphore_signal(near_sem, inc=1, device_id=peer, device_id_type=MESH)

    def tell(step):
        for to in ((z + step) % nz, (z + nz - step) % nz):
            pl.semaphore_signal(far_sem.at[step.bit_length() - 1], inc=1, device_id=z_id(to), device_id_type=MESH)

    def hear(step):
        pl.semaphore_wait(far_sem.at[step.bit_length() - 1], 2)

    steps = [1 << e for e in range(8) if 2 * (1 << e) <= nz // 2]
    if steps:
        tell(steps[0])

    def pick_local(k, carry):
        sel = one_hot(place == cc_ref[pl.ds(k, 1), :])
        got = dot(xt_ref[0], sel) + dot(xt_ref[1], sel) + dot(xt_ref[2], sel)
        pick_ref[k] = got.reshape(BLOCK, LOADS, BROWS_DEV)
        return carry

    lax.fori_loop(1, SLOTS, pick_local, 0)
    load_s.wait()
    if len(steps) > 1:
        hear(steps[0])
        tell(steps[1])

    def multiply(k, source, start):
        for c in range(2):
            lanes = slice(128 * c, 128 * (c + 1))
            for h in range(2):
                loads = slice(32 * h, 32 * (h + 1))
                total = None if start else acc_ref[:, loads, lanes]
                for j in range(BLOCK):
                    term = s_ref[k, :, j : j + 1, lanes] * source(j, loads, lanes)[None]
                    total = term if total is None else total + term
                acc_ref[:, loads, lanes] = total

    multiply(0, lambda j, loads, lanes: x_ref[j, loads, lanes], True)

    r = iota((BROWS_DEV, 192), 0)
    n = iota((BROWS_DEV, 192), 1)
    for q in range(4):
        want = (n % 64) // SEND * 128 + SEND * q + n % SEND
        for t in range(3):
            sel_ref[q, t] = one_hot(jnp.logical_and(n // 64 == t, r == want))

    ghost_place = BROWS_DEV + iota((192, BROWS_DEV), 0) % 64

    to_prev.wait_recv()
    to_next.wait_recv()
    sides = [split3(halo_in[0]), split3(halo_in[1])]
    for q in range(4):
        total = None
        for t in range(3):
            term = dot(sides[0][t], sel_ref[q, t, :128]) + dot(sides[1][t], sel_ref[q, t, 128:])
            total = term if total is None else total + term
        gst_ref[128 * q : 128 * (q + 1), :] = total.astype(BF16)

    def add_ghosts(k, carry):
        sel = one_hot(ghost_place == cc_ref[k : k + 1, :])
        got = dot(gst_ref[...], sel).reshape(BLOCK, LOADS, BROWS_DEV)
        pick_ref[k] = pick_ref[k] + got
        return carry

    for k in range(1, SLOTS):
        add_ghosts(k, 0)
    for c in range(2):
        lanes = slice(128 * c, 128 * (c + 1))

        for h in range(LOADS // 16):
            loads = slice(16 * h, 16 * (h + 1))

            def slot(k, total):
                for j in range(BLOCK):
                    total = total + s_ref[k, :, j : j + 1, lanes] * pick_ref[k, j, loads, lanes][None]
                return total

            acc_ref[:, loads, lanes] = lax.fori_loop(1, SLOTS, slot, acc_ref[:, loads, lanes])
        if c == 0 and len(steps) > 2:
            hear(steps[1])
            tell(steps[2])

    gram = None
    for i in range(BLOCK):
        scaled = acc_ref[i] / s_ref[0, i, i : i + 1, :]
        wt_ref[i] = jnp.concatenate(split3(scaled), axis=0)
        term = lax.dot_general(wt_ref[i], wt_ref[i], (((1,), (1,)), ((), ())),
                               preferred_element_type=F32)
        gram = term if gram is None else gram + term
    gram = gram[0:64] + gram[64:128] + gram[128:192]
    gram = gram[:, 0:64] + gram[:, 64:128] + gram[:, 128:192]
    gram = gram * (1.0 / (BLOCK * BROWS_DEV * slabs))

    pack(plane_out, gram)
    pl.semaphore_wait(near_sem, nx - 1)
    plane_in[me_plane] = plane_out[core]

    def send_plane(to_x, to_sub, wanted):
        @pl.when(wanted)
        def _():
            pltpu.make_async_remote_copy(
                src_ref=plane_out.at[to_sub % 2], dst_ref=plane_in.at[me_plane],
                send_sem=plane_sem.at[0], recv_sem=plane_sem.at[1],
                device_id=(z * nx + to_x, to_sub), device_id_type=MESH).start()

    for to_sub in (0, 1):
        send_plane(0, to_sub, me_plane != to_sub)
    for dx in (2, 1, 3, 0):
        for dy in range(ny2):
            shift = (ny2 // 2 + dy) % ny2
            if dx or shift:
                to_x, to_sub = (x + dx) % nx, (sub + shift) % ny2
                send_plane(to_x, to_sub, to_x * ny2 + to_sub >= 2)

    part = plane_in.at[pl.ds(0, nplane - 1)]
    plane_all = pltpu.make_async_remote_copy(
        src_ref=part, dst_ref=part, send_sem=plane_sem.at[0], recv_sem=plane_sem.at[1],
        device_id=(rows, sub + 1 - 2 * core), device_id_type=MESH)
    plane_all.wait_recv()
    total = jnp.sum(plane_in[...], axis=0)
    z_out[...] = total
    z_in[z] = total

    if steps:
        hear(steps[-1])

    is_mate = jnp.logical_and(rows == 0, sub == 0)
    direct = pltpu.make_async_remote_copy(
        src_ref=z_out, dst_ref=direct_in.at[z], send_sem=direct_sem.at[0], recv_sem=direct_sem.at[1],
        device_id=(0, 1), device_id_type=MESH)

    @pl.when(is_source)
    def _():
        direct.start()

    def send_z(q, carry):
        half = (q + 1) // 2
        to = (z + nz // 2 + half * (1 - 2 * (q % 2))) % nz
        pltpu.make_async_remote_copy(
            src_ref=z_out, dst_ref=z_in.at[z], send_sem=z_sem.at[0],
            recv_sem=z_sem.at[1], device_id=z_id(to), device_id_type=MESH).start()
        return carry

    lax.fori_loop(0, nz - 1, send_z, 0)
    part = z_in.at[pl.ds(0, nz - 1)]
    z_all = pltpu.make_async_remote_copy(
        src_ref=part, dst_ref=part, send_sem=z_sem.at[0], recv_sem=z_sem.at[1],
        device_id=z_id((z + 1) % nz), device_id_type=MESH)
    z_all.wait_recv()
    total = jnp.sum(z_in[...], axis=0)
    core_out[...] = total
    sum_ref[core] = total
    to_core = pltpu.make_async_remote_copy(
        src_ref=core_out, dst_ref=sum_ref.at[core], send_sem=core_sem.at[0],
        recv_sem=core_sem.at[1], device_id=(rows, sub + 1 - 2 * core), device_id_type=MESH)

    @pl.when(jnp.logical_not(is_mate))
    def _():
        to_core.start()

    @pl.when(jnp.logical_not(is_first))
    def _():
        to_core.wait_recv()

    @pl.when(is_first)
    def _():
        pltpu.make_async_remote_copy(
            src_ref=direct_in, dst_ref=direct_in, send_sem=direct_sem.at[0], recv_sem=direct_sem.at[1],
            device_id=(0, 0), device_id_type=MESH).wait_recv()
        sum_ref[0] = jnp.sum(direct_in[...], axis=0)


    to_prev.wait_send()
    to_next.wait_send()
    plane_all.wait_send()
    z_all.wait_send()

    @pl.when(is_source)
    def _():
        direct.wait_send()

    @pl.when(jnp.logical_not(is_mate))
    def _():
        to_core.wait_send()


def pack(ref, gram):
    wide = [gram[0:16], jnp.concatenate([gram[16:32, 16:64], gram[32:48, 32:48]], axis=1)]
    small = [gram[48:64, 48:64], gram[32:48, 48:64]]
    for c in range(2):
        ref[c, 0:8, :] = jnp.concatenate([wide[c][0:8], wide[c][8:16]], axis=1)
        ref[c, 8:10, :] = jnp.concatenate([small[c][2 * i : 2 * i + 2] for i in range(8)], axis=1)


def unpack(ref):
    wide = [jnp.concatenate([ref[c, 0:8, 0:64], ref[c, 0:8, 64:128]], axis=0) for c in range(2)]
    small = [jnp.concatenate([ref[c, 8:10, 16 * i : 16 * (i + 1)] for i in range(8)], axis=0) for c in range(2)]
    zeros = jnp.zeros((16, 48), F32)
    rows = [
        wide[0],
        jnp.concatenate([zeros[:, 0:16], wide[1][:, 0:48]], axis=1),
        jnp.concatenate([zeros[:, 0:32], wide[1][:, 48:64], small[1]], axis=1),
        jnp.concatenate([zeros, small[0]], axis=1),
    ]
    upper = jnp.concatenate(rows, axis=0)
    keep = iota((LOADS, LOADS), 0) <= iota((LOADS, LOADS), 1)
    return jnp.where(keep, upper, upper.T)


def apply_kernel(wt_ref, sum_ref, out_hbm, factor_hbm, out_ref, factor_ref, rows_ref, cols_ref, near_ref, sems):
    gram = unpack(sum_ref)
    on_diagonal = iota((LOADS, LOADS), 0) == iota((LOADS, LOADS), 1)
    diagonal = jnp.where(on_diagonal, gram, 0.0)
    square = jnp.sum(diagonal, axis=0, keepdims=True)
    lane_scale = lax.rsqrt(square)
    row_scale = lax.rsqrt(jnp.sum(diagonal, axis=1, keepdims=True))
    both = jnp.concatenate([gram * row_scale * lane_scale, jnp.where(on_diagonal, lane_scale, 0.0)], axis=1)
    outs = factor_rows([both[8 * p : 8 * p + 8] for p in range(8)], cols_ref, near_ref)
    for p in range(8):
        for j in range(8):
            rows_ref[8 * p + j : 8 * p + j + 1, :] = outs[p][j][0:1]
    found = rows_ref[...]
    upper = iota((LOADS, LOADS), 0) <= iota((LOADS, LOADS), 1)
    factor_ref[...] = jnp.where(upper, found[:, :LOADS] * (square * lane_scale), 0.0)
    store = pltpu.make_async_copy(factor_ref, factor_hbm, sems.at[BLOCK])
    store.start()
    stores = [store]
    left = jnp.concatenate([jnp.concatenate([term] * 3, axis=1) for term in split3(found[:, LOADS:])], axis=0)
    for i in range(BLOCK):
        got = dot(left, wt_ref[i])
        out_ref[i] = got[0:64] + got[64:128] + got[128:192]
        store = pltpu.make_async_copy(out_ref.at[i], out_hbm.at[i], sems.at[i])
        store.start()
        stores.append(store)
    for store in stores:
        store.wait()


def on_device(nz, ny2, basis, stiffness, col_index, block_count, send_list):
    nplane = CHIPS_X * ny2
    vmem = pl.BlockSpec(memory_space=pltpu.VMEM)
    hbm = pl.BlockSpec(memory_space=pltpu.MemorySpace.HBM)
    held = [
        pltpu.with_memory_space_constraint(value, pltpu.MemorySpace.HBM)
        for value in (basis, stiffness, col_index, block_count.reshape(1, BROWS_DEV), send_list)
    ]
    wt, total = pl.pallas_call(
        functools.partial(kernel, nz, ny2),
        out_shape=(
            jax.ShapeDtypeStruct((BLOCK, 3 * LOADS, BROWS_DEV), BF16),
            jax.ShapeDtypeStruct((2, 10, 128), F32),
        ),
        in_specs=[hbm, hbm, hbm, hbm, hbm],
        out_specs=(vmem, vmem),
        scratch_shapes=[
            pltpu.VMEM((BLOCK, LOADS, BROWS_DEV), F32),
            pltpu.VMEM((SLOTS, BLOCK, BLOCK, BROWS_DEV), F32),
            pltpu.VMEM((SLOTS, BROWS_DEV), jnp.int32),
            pltpu.VMEM((1, BROWS_DEV), jnp.int32),
            pltpu.VMEM((2, SEND), jnp.int32),
            pltpu.VMEM((3, BLOCK * LOADS, BROWS_DEV), BF16),
            pltpu.VMEM((SLOTS, BROWS_DEV), jnp.int32),
            pltpu.VMEM((SLOTS, BLOCK, LOADS, BROWS_DEV), F32),
            pltpu.VMEM((BLOCK, LOADS, BROWS_DEV), F32),
            pltpu.VMEM((BLOCK * LOADS, 192), BF16),
            pltpu.VMEM((4, 3, BROWS_DEV, 192), BF16),
            pltpu.VMEM((SLOTS, 192, BROWS_DEV), BF16),
            pltpu.VMEM((2, 128, 128), F32),
            pltpu.VMEM((2, 128, 128), F32),
            pltpu.VMEM((2, 10, 128), F32),
            pltpu.VMEM((nplane, 10, 128), F32),
            pltpu.VMEM((10, 128), F32),
            pltpu.VMEM((nz, 10, 128), F32),
            pltpu.VMEM((10, 128), F32),
            pltpu.VMEM((nz, 10, 128), F32),
            pltpu.SemaphoreType.DMA((5,)),
            pltpu.SemaphoreType.DMA((4,)),
            pltpu.SemaphoreType.DMA((2,)),
            pltpu.SemaphoreType.DMA((2,)),
            pltpu.SemaphoreType.DMA((2,)),
            pltpu.SemaphoreType.REGULAR,
            pltpu.SemaphoreType.REGULAR((4,)),
            pltpu.SemaphoreType.DMA((2,)),
        ],
        name="arnoldi_step",
        compiler_params=pltpu.CompilerParams(
            collective_id=1, has_side_effects=True, vmem_limit_bytes=40 * 1024 * 1024),
    )(*held)
    return pl.pallas_call(
        apply_kernel,
        out_shape=(jax.ShapeDtypeStruct(basis.shape, F32), jax.ShapeDtypeStruct((LOADS, LOADS), F32)),
        in_specs=[vmem, vmem],
        out_specs=(hbm, hbm),
        scratch_shapes=[
            pltpu.VMEM((BLOCK, LOADS, BROWS_DEV), F32),
            pltpu.VMEM((LOADS, LOADS), F32),
            pltpu.VMEM((LOADS, 128), F32),
            pltpu.VMEM((8, 9, 8, 128), F32),
            pltpu.VMEM((8, 8, 8, 128), F32),
            pltpu.SemaphoreType.DMA((BLOCK + 1,)),
        ],
        name="apply",
        compiler_params=pltpu.CompilerParams(vmem_limit_bytes=16 * 1024 * 1024),
    )(wt, total)


def solution(mesh):
    nz, ny2 = mesh.shape["rows"] // CHIPS_X, mesh.shape["sub"]
    in_specs = (
        P(None, None, ("rows", "sub")),
        P(None, None, None, ("rows", "sub")),
        P(None, ("rows", "sub")),
        P(("rows", "sub")),
        P(None, ("rows", "sub")),
    )
    out_specs = (P(None, None, ("rows", "sub")), P())
    return jax.shard_map(
        functools.partial(on_device, nz, ny2), mesh=mesh, in_specs=in_specs, out_specs=out_specs,
        check_vma=False,
    )
```
